128 devices in a mesh: ctx: 16 (over y_hi, z, core), dp: 8 (over x, y_lo).
Axes of the slice: x: 4, y: 4 (y_hi: 2, y_lo: 2; y = y_hi * 2 + y_lo), z: 4, core: 2. Of those that a mesh axis runs over, the one named last changes fastest.
Arguments:
- query_rows: bfloat16 [8, 2048, 4096], P(None, ('ctx', 'dp')), may hold values from -28 to 28
- key_rows: bfloat16 [8, 2048, 512], P(None, ('ctx', 'dp')), may hold values from -28 to 28
- value_rows: bfloat16 [8, 2048, 512], P(None, ('ctx', 'dp')), may hold values from -4 to 4
- out_grad: bfloat16 [8, 2048, 4096], P(None, ('ctx', 'dp')), may hold values from -6 to 6
- doc_lengths: int32 [8, 8], replicated, may hold values from 1 to 1024, 2048 in all within a row
- assignment: int32 [8], replicated, may hold values from 0 to 7, each once
Outputs:
- query_grad: bfloat16 [8, 2048, 4096], P('dp', 'ctx')
- key_grad: bfloat16 [8, 2048, 512], P('dp', 'ctx')
- value_grad: bfloat16 [8, 2048, 512], P('dp', 'ctx')
The draws below stay inside these ranges and needn't reach their ends.
Inputs may be any that keep to these rules, and one draw needn't show every extreme that they name: `doc_lengths`: each row lists the 8 documents packed in order into one sequence; they sum to 2048 and the longest holds exactly 1024 tokens. `assignment`: A permutation of the sequences.
All inputs are finite; a program needn't handle non-finite values.
Results may differ from the reference program's by a relative error of at most 0.022.
Values may be sent and summed in bfloat16 or wider, within the bound.
No kernel may reach another device: no remote copies, remote signals or barrier semaphores. Data moves between devices by JAX's collectives and lax.ppermute only.
A program may use at most 128 MiB of HBM per device.

```python
import math
import jax
import jax.numpy as jnp
import numpy as np
from jax import lax

HQ = 32
HK = 4
DH = 128
NDOC = 8
SEQS = 8
LEN = 2048


def draw_key_rows(key, part):
    key = jax.random.fold_in(key, 3)
    drawn = jnp.clip(jax.random.normal(key, (SEQS, LEN, HK * DH)), -4.0, 4.0)
    return drawn.astype(jnp.bfloat16)


def draw_query_rows(key, part):
    key = jax.random.fold_in(key, 5)
    drawn = jnp.clip(jax.random.normal(key, (SEQS, LEN, HQ * DH)), -4.0, 4.0)
    return drawn.astype(jnp.bfloat16)


def level_of(stream_key, dims, split, low, largest):
    def one(dim, blocks):
        steps = jax.random.uniform(jax.random.fold_in(jax.random.fold_in(stream_key, 6), dim), (blocks,), jnp.float32, low / len(split), largest / len(split))
        return jnp.repeat(jnp.exp(steps), dims[dim] // blocks).reshape((-1,) + (1,) * (len(dims) - dim - 1))

    level = one(*split[0])
    for cut in split[1:]:
        level = level * one(*cut)
    return level


def profile(count, total, limit, lean):
    weights = [(1 << 20) // math.isqrt(standing ** lean) + 1 for standing in range(2, count + 1)]
    rest, holding = total - limit - (count - 1), [1] * (count - 1)
    while rest > 0:
        free = [i for i in range(count - 1) if holding[i] < limit]
        whole, budget = sum([weights[i] for i in free]), rest
        for i in free:
            addition = min(limit - holding[i], max(1, budget * weights[i] // whole), rest)
            holding[i] = holding[i] + addition
            rest = rest - addition
    return np.array([limit] + holding)


def ragged_sizes(own_key, count, total, most, lean):
    if count == 2:
        one = jax.random.randint(own_key, (), max(1, total - most), min(most, total - 1) + 1)
        return jnp.stack([one, total - one])
    tallies = jnp.asarray(profile(count, total, most, lean), jnp.int32)
    couples = (count - 1) // 2
    donor, taker = tallies[1:1 + 2 * couples:2], tallies[2:2 + 2 * couples:2]
    margin = jnp.minimum(donor - 1, most - taker)
    passed = jax.random.randint(jax.random.fold_in(own_key, 1), (couples,), 0, 1 << 20) % (margin + 1)
    tallies = tallies.at[1:1 + 2 * couples:2].set(donor - passed).at[2:2 + 2 * couples:2].set(taker + passed)
    return tallies[jax.random.permutation(jax.random.fold_in(own_key, 2), count)]


def noise(key, extent, deviation, most, shards=(), held_as=jnp.bfloat16):
    values = deviation * jax.random.normal(key, extent, jnp.float32)
    if shards:
        values = values * level_of(key, extent, shards, -0.22, 0.18)
    return jnp.clip(values, -most, most).astype(held_as)


def setup_inputs(seed: int = 0) -> dict:
    seeds = jax.random.split(jax.random.key(seed), 7)
    return {
        "query_rows": draw_query_rows(jax.random.fold_in(seeds[6], 71), 0),
        "key_rows": draw_key_rows(jax.random.fold_in(seeds[6], 71), 0),
        "value_rows": noise(seeds[2], (SEQS, LEN, HK * DH), 1.0, 4.0, ((1, 128),)),
        "out_grad": noise(seeds[3], (SEQS, LEN, HQ * DH), 1.0, 6.0, ((1, 128),)),
        "doc_lengths": jax.vmap(lambda own: ragged_sizes(own, NDOC, LEN, LEN // 2, 2))(jax.random.split(seeds[4], SEQS)).reshape((SEQS, NDOC)).astype(jnp.int32),
        "assignment": jax.random.permutation(seeds[5], SEQS).astype(jnp.int32),
    }


masked_score = -1.0e30


def document_ids(places, doc_ends):
    return jnp.sum((places[:, None] >= doc_ends[None, :]).astype(jnp.int32), axis=1)


def rounded(values_in):
    held = values_in.astype(jnp.bfloat16)
    held = lax.optimization_barrier(held)
    return held.astype(jnp.float32)


def reference(query_rows, key_rows, value_rows, out_grad, doc_lengths, assignment):
    group_size = HQ // HK
    softmax_scale = DH ** -0.5
    highest = lax.Precision.HIGHEST
    places = jnp.arange(LEN, dtype=jnp.int32)

    def one_group(group_index):
        chosen = assignment[group_index].astype(jnp.int32)
        queries_seq = lax.dynamic_index_in_dim(query_rows, chosen, 0, keepdims=False)
        keys_seq = lax.dynamic_index_in_dim(key_rows, chosen, 0, keepdims=False)
        values_seq = lax.dynamic_index_in_dim(value_rows, chosen, 0, keepdims=False)
        grads_seq = lax.dynamic_index_in_dim(out_grad, chosen, 0, keepdims=False)
        length_row = lax.dynamic_index_in_dim(doc_lengths, chosen, 0, keepdims=False)
        doc_ids = document_ids(places, jnp.cumsum(length_row).astype(jnp.int32))
        allowed = (places[None, :] <= places[:, None]) & (doc_ids[None, :] == doc_ids[:, None])

        def one_head(head_index):
            query_head = lax.dynamic_slice_in_dim(queries_seq, head_index * group_size * DH, group_size * DH, 1)
            query_head = query_head.astype(jnp.float32).reshape(LEN, group_size, DH)
            grad_head = lax.dynamic_slice_in_dim(grads_seq, head_index * group_size * DH, group_size * DH, 1)
            grad_head = grad_head.astype(jnp.float32).reshape(LEN, group_size, DH)
            key_head = lax.dynamic_slice_in_dim(keys_seq, head_index * DH, DH, 1).astype(jnp.float32)
            value_head = lax.dynamic_slice_in_dim(values_seq, head_index * DH, DH, 1).astype(jnp.float32)
            scores = jnp.einsum("qgd,kd->gqk", query_head, key_head, precision=highest) * softmax_scale
            scores = jnp.where(allowed[None], scores, masked_score)
            row_peak = jnp.max(scores, axis=-1, keepdims=True)
            row_lse = row_peak + jnp.log(jnp.sum(jnp.exp(scores - row_peak), axis=-1, keepdims=True))
            probs = jnp.where(allowed[None], jnp.exp(scores - row_lse), 0.0)
            attended = jnp.einsum("gqk,kd->qgd", probs, value_head, precision=highest)
            row_delta = jnp.sum(grad_head * attended, axis=-1)
            probs_low = rounded(probs)
            value_grad = jnp.einsum("gqk,qgd->kd", probs_low, grad_head, precision=highest)
            prob_grad = jnp.einsum("qgd,kd->gqk", grad_head, value_head, precision=highest)
            score_grad = rounded(probs * (prob_grad - jnp.transpose(row_delta)[:, :, None]))
            query_grad = jnp.einsum("gqk,kd->qgd", score_grad, key_head, precision=highest) * softmax_scale
            key_grad = jnp.einsum("gqk,qgd->kd", score_grad, query_head, precision=highest) * softmax_scale
            return query_grad.reshape(LEN, group_size * DH), key_grad, value_grad

        query_all, key_all, value_all = lax.map(one_head, jnp.arange(HK, dtype=jnp.int32))
        query_all = jnp.transpose(query_all, (1, 0, 2)).reshape(LEN, HQ * DH)
        key_all = jnp.transpose(key_all, (1, 0, 2)).reshape(LEN, HK * DH)
        value_all = jnp.transpose(value_all, (1, 0, 2)).reshape(LEN, HK * DH)
        return (query_all.astype(jnp.bfloat16), key_all.astype(jnp.bfloat16), value_all.astype(jnp.bfloat16))

    query_grad, key_grad, value_grad = lax.map(one_group, jnp.arange(SEQS, dtype=jnp.int32))
    return (query_grad, key_grad, value_grad)
```

```python
import functools
import math

import jax
import jax.numpy as jnp
from jax import lax
from jax.experimental import pallas as pl
from jax.experimental.pallas import tpu as pltpu
from jax.sharding import PartitionSpec as P

HQ = 32
HK = 4
DH = 128
NDOC = 8
LEN = 2048
GROUP = HQ // HK

CTX = 16
DP = 8
ROWS = LEN // (CTX * DP)
OWN = LEN // CTX
HEADS = HQ // CTX
QW = HEADS * DH
SHARE = CTX // HK
IN_W = 2 * QW + 2 * DH
OUT_W = QW + 2 * DH

TQ = 256
TK = 256
NKB = LEN // TK

SCALE = DH ** (-0.5)
LOG2E = math.log2(math.e)
MASKED = -1e30
F32 = jnp.float32
BF16 = jnp.bfloat16
MIB = 1024 * 1024


def pack_kernel(seq_ref, q_ref, g_ref, k_ref, v_ref, out_ref):
    for group in range(DP):
        seq = seq_ref[group]
        for part in range(SHARE):
            cols = slice(part * QW, (part + 1) * QW)
            slot = part * DP + group
            out_ref[slot, :, 0:QW] = q_ref[seq, :, cols]
            out_ref[slot, :, QW : 2 * QW] = g_ref[seq, :, cols]
            out_ref[slot, :, 2 * QW : 2 * QW + DH] = k_ref[seq]
            out_ref[slot, :, 2 * QW + DH : IN_W] = v_ref[seq]


def pack(assignment, query_rows, out_grad, key_rows, value_rows):
    wide = pl.BlockSpec((DP, ROWS, SHARE * QW), lambda j, seq: (0, 0, j))
    thin = pl.BlockSpec((DP, ROWS, DH), lambda j, seq: (0, 0, j))
    return pl.pallas_call(
        pack_kernel,
        out_shape=jax.ShapeDtypeStruct((CTX * DP, ROWS, IN_W), BF16),
        grid_spec=pltpu.PrefetchScalarGridSpec(
            num_scalar_prefetch=1,
            grid=(HK,),
            in_specs=[wide, wide, thin, thin],
            out_specs=pl.BlockSpec((SHARE * DP, ROWS, IN_W), lambda j, seq: (j, 0, 0)),
        ),
        compiler_params=pltpu.CompilerParams(vmem_limit_bytes=24 * MIB),
        name="pack",
    )(assignment, query_rows, out_grad, key_rows, value_rows)


def attention_kernel(
    group_ref, seq_ref, len_ref, qg_ref, kv_ref, out_ref, kt_ref, e_ref, dp_ref, top_ref, dk_ref, dv_ref
):
    step = pl.program_id(0)
    width = HEADS * TQ
    seq = seq_ref[group_ref[0]]

    @pl.when(step == 0)
    def _():
        dk_ref[...] = jnp.zeros_like(dk_ref)
        dv_ref[...] = jnp.zeros_like(dv_ref)
        for b in range(NKB):
            kt_ref[b] = kv_ref[b * TK : (b + 1) * TK, 0:DH].T

    first = step * TQ
    place = first + lax.broadcasted_iota(jnp.int32, (1, TQ), 1)
    begin = jnp.zeros((1, TQ), jnp.int32)
    first_begin = jnp.int32(0)
    end = jnp.int32(0)
    for j in range(NDOC):
        end = end + len_ref[seq, j]
        begin = jnp.where(place >= end, end, begin)
        first_begin = jnp.where(first >= end, end, first_begin)
    place = jnp.concatenate([place] * HEADS, axis=1)
    begin = jnp.concatenate([begin] * HEADS, axis=1)
    low = first_begin // TK
    high = (first + TQ - 1) // TK + 1

    q_rows = jnp.concatenate([qg_ref[:, h * DH : (h + 1) * DH] for h in range(HEADS)], axis=0)
    g_rows = jnp.concatenate(
        [qg_ref[:, QW + h * DH : QW + (h + 1) * DH] for h in range(HEADS)], axis=0
    )
    q_cols = q_rows.T
    g_cols = g_rows.T

    def statistics(b, state):
        top, mass, weighted = state
        rows = pl.ds(pl.multiple_of(b * TK, TK), TK)
        s = jnp.dot(kv_ref[rows, 0:DH], q_cols, preferred_element_type=F32) * (SCALE * LOG2E)
        dp = jnp.dot(kv_ref[rows, DH : 2 * DH], g_cols, preferred_element_type=F32)
        u = b * TK + lax.broadcasted_iota(jnp.int32, (TK, width), 0)
        s = jnp.where((u <= place) & (u >= begin), s, MASKED)
        new_top = jnp.maximum(top, jnp.max(s, axis=0, keepdims=True))
        keep = jnp.exp2(top - new_top)
        e = jnp.exp2(s - new_top)
        e_ref[b] = e
        dp_ref[b] = dp
        top_ref[b] = new_top
        mass = mass * keep + jnp.sum(e, axis=0, keepdims=True)
        weighted = weighted * keep + jnp.sum(e * dp, axis=0, keepdims=True)
        return new_top, mass, weighted

    zero = jnp.zeros((1, width), F32)
    top, mass, weighted = lax.fori_loop(
        low, high, statistics, (jnp.full((1, width), MASKED, F32), zero, zero)
    )
    inverse = 1.0 / mass
    delta = weighted * inverse

    def gradients(b, dq):
        rows = pl.ds(pl.multiple_of(b * TK, TK), TK)
        probs = e_ref[b] * (jnp.exp2(top_ref[b] - top) * inverse)
        low_probs = probs.astype(BF16)
        ds = (probs * (dp_ref[b] - delta)).astype(BF16)
        dv_ref[rows, :] += jnp.dot(low_probs, g_rows, preferred_element_type=F32)
        dk_ref[rows, :] += jnp.dot(ds, q_rows, preferred_element_type=F32)
        return dq + jnp.dot(kt_ref[b], ds, preferred_element_type=F32)

    dq = lax.fori_loop(low, high, gradients, jnp.zeros((DH, width), F32))
    dq = (dq * SCALE).T.astype(BF16)
    out_rows = pl.ds(pl.multiple_of(first, TQ), TQ)
    for h in range(HEADS):
        out_ref[out_rows, h * DH : (h + 1) * DH] = dq[h * TQ : (h + 1) * TQ]

    @pl.when(step == pl.num_programs(0) - 1)
    def _():
        out_ref[:, QW : QW + DH] = (dk_ref[...] * SCALE).astype(BF16)
        out_ref[:, QW + DH : OUT_W] = dv_ref[...].astype(BF16)


def attention(own_group, assignment, doc_lengths, rows):
    width = HEADS * TQ
    return pl.pallas_call(
        attention_kernel,
        out_shape=jax.ShapeDtypeStruct((LEN, OUT_W), BF16),
        grid_spec=pltpu.PrefetchScalarGridSpec(
            num_scalar_prefetch=3,
            grid=(LEN // TQ,),
            in_specs=[
                pl.BlockSpec((TQ, 2 * QW), lambda i, *_: (i, 0)),
                pl.BlockSpec((LEN, 2 * DH), lambda i, *_: (0, 2)),
            ],
            out_specs=pl.BlockSpec((LEN, OUT_W), lambda i, *_: (0, 0)),
            scratch_shapes=[
                pltpu.VMEM((NKB, DH, TK), BF16),
                pltpu.VMEM((NKB, TK, width), F32),
                pltpu.VMEM((NKB, TK, width), F32),
                pltpu.VMEM((NKB, 1, width), F32),
                pltpu.VMEM((LEN, DH), F32),
                pltpu.VMEM((LEN, DH), F32),
            ],
        ),
        compiler_params=pltpu.CompilerParams(vmem_limit_bytes=40 * MIB),
        name="attention",
    )(own_group, assignment, doc_lengths, rows, rows)


def unpack_kernel(in_ref, dq_ref, dk_ref, dv_ref):
    dk = jnp.zeros((OWN, DH), F32)
    dv = jnp.zeros((OWN, DH), F32)
    for part in range(SHARE):
        dq_ref[0, :, part * QW : (part + 1) * QW] = in_ref[part, :, 0:QW]
        dk = dk + in_ref[part, :, QW : QW + DH].astype(F32)
        dv = dv + in_ref[part, :, QW + DH : OUT_W].astype(F32)
    dk_ref[0] = dk.astype(BF16)
    dv_ref[0] = dv.astype(BF16)


def unpack(blocks):
    return pl.pallas_call(
        unpack_kernel,
        out_shape=(
            jax.ShapeDtypeStruct((1, OWN, HQ * DH), BF16),
            jax.ShapeDtypeStruct((1, OWN, HK * DH), BF16),
            jax.ShapeDtypeStruct((1, OWN, HK * DH), BF16),
        ),
        grid=(HK,),
        in_specs=[pl.BlockSpec((SHARE, OWN, OUT_W), lambda j: (j, 0, 0))],
        out_specs=(
            pl.BlockSpec((1, OWN, SHARE * QW), lambda j: (0, 0, j)),
            pl.BlockSpec((1, OWN, DH), lambda j: (0, 0, j)),
            pl.BlockSpec((1, OWN, DH), lambda j: (0, 0, j)),
        ),
        name="unpack",
    )(blocks)


def local(query_rows, key_rows, value_rows, out_grad, doc_lengths, assignment):
    own_group = lax.axis_index("dp").astype(jnp.int32).reshape(1)
    sent = pack(assignment, query_rows, out_grad, key_rows, value_rows)
    got = lax.all_to_all(sent, ("ctx", "dp"), split_axis=0, concat_axis=0, tiled=True)
    grads = attention(own_group, assignment, doc_lengths, got.reshape(LEN, IN_W))
    back = lax.all_to_all(
        grads.reshape(CTX, OWN, OUT_W), "ctx", split_axis=0, concat_axis=0, tiled=True
    )
    return unpack(back)


def solution(mesh):
    placed = (
        P(None, ("ctx", "dp"), None),
        P(None, ("ctx", "dp"), None),
        P(None, ("ctx", "dp"), None),
        P(None, ("ctx", "dp"), None),
        P(),
        P(),
    )
    return jax.shard_map(
        local,
        mesh=mesh,
        in_specs=placed,
        out_specs=(P("dp", "ctx", None), P("dp", "ctx", None), P("dp", "ctx", None)),
        check_vma=False,
    )
```

```python
import functools
import math

import jax
import jax.numpy as jnp
from jax import lax
from jax.experimental import pallas as pl
from jax.experimental.pallas import tpu as pltpu
from jax.sharding import PartitionSpec as P

HQ = 32
HK = 4
DH = 128
NDOC = 8
LEN = 2048
GROUP = HQ // HK

CTX = 16
DP = 8
ROWS = LEN // (CTX * DP)
OWN = LEN // CTX
CORES = 2
HEADS = HQ // CTX
QW = HEADS * DH
SHARE = CTX // HK
IN_W = 2 * QW + DH
OUT_W = QW + 2 * DH

PIECE = 32
TQ = 256
TK = 256
NKB = LEN // TK
MOST = min(NKB, (LEN // 2 + TQ - 2) // TK + 1)
SUB = 128

SCALE = DH ** (-0.5)
LOG2E = math.log2(math.e)
MASKED = -1e30
F32 = jnp.float32
BF16 = jnp.bfloat16
MIB = 1024 * 1024


def pack_kernel(seq_ref, q_in, g_in, k_in, v_in, out, q_ref, g_ref, k_ref, v_ref, out_ref, in_sem, out_sem):
    wide = SHARE * QW
    slots = SHARE * DP

    def load(j, a, source, held, thin):
        width = DH if thin else wide
        cols = slice(j * width, (j + 1) * width)
        return pltpu.make_async_copy(source.at[:, :, cols], held.at[:, :, cols], in_sem.at[j, a])

    loads = [
        [load(j, 0, q_in, q_ref, False), load(j, 1, g_in, g_ref, False), load(j, 2, k_in, k_ref, True), load(j, 3, v_in, v_ref, True)]
        for j in range(HK)
    ]
    for group in loads:
        for move in group:
            move.start()
    stores = []
    for j in range(HK):
        for move in loads[j]:
            move.wait()
        for part in range(SHARE):
            cols = slice(j * wide + part * QW, j * wide + (part + 1) * QW)
            thin = slice(j * DH, (j + 1) * DH)
            first = (j * SHARE + part) * DP
            for group in range(DP):
                seq = seq_ref[group]
                out_ref[first + group, :, 0:QW] = q_ref[seq, :, cols]
                out_ref[first + group, :, QW : 2 * QW] = g_ref[seq, :, cols]
                out_ref[first + group, :, 2 * QW : IN_W] = (v_ref if part % CORES else k_ref)[seq, :, thin]
            rows = slice(first, first + DP)
            move = pltpu.make_async_copy(out_ref.at[rows], out.at[rows], out_sem.at[j * SHARE + part])
            move.start()
            stores.append(move)
    for move in stores:
        move.wait()


def pack(assignment, query_rows, out_grad, key_rows, value_rows):
    whole = pl.BlockSpec(memory_space=pl.ANY)
    return pl.pallas_call(
        pack_kernel,
        out_shape=jax.ShapeDtypeStruct((CTX * DP, ROWS, IN_W), BF16),
        in_specs=[pl.BlockSpec(memory_space=pltpu.SMEM)] + [whole] * 4,
        out_specs=whole,
        scratch_shapes=[
            pltpu.VMEM((DP, ROWS, HQ * DH), BF16),
            pltpu.VMEM((DP, ROWS, HQ * DH), BF16),
            pltpu.VMEM((DP, ROWS, HK * DH), BF16),
            pltpu.VMEM((DP, ROWS, HK * DH), BF16),
            pltpu.VMEM((CTX * DP, ROWS, IN_W), BF16),
            pltpu.SemaphoreType.DMA((HK, 4)),
            pltpu.SemaphoreType.DMA((CTX,)),
        ],
        compiler_params=pltpu.CompilerParams(vmem_limit_bytes=60 * MIB),
        name="pack",
    )(assignment, query_rows, out_grad, key_rows, value_rows)


def attention_kernel(
    own_ref, seq_ref, len_ref, qg_ref, mine_ref, other_ref, out_ref, k_ref, v_ref, kt_ref, e_ref, dp_ref, dk_ref, dv_ref
):
    step = pl.program_id(0)
    width = HEADS * TQ
    seq = seq_ref[own_ref[0]]
    has_key = own_ref[1] == 0

    @pl.when((step == 0) & has_key)
    def _():
        k_ref[...] = mine_ref[...]
        v_ref[...] = other_ref[...]

    @pl.when((step == 0) & jnp.logical_not(has_key))
    def _():
        k_ref[...] = other_ref[...]
        v_ref[...] = mine_ref[...]

    @pl.when(step == 0)
    def _():
        dk_ref[...] = jnp.zeros_like(dk_ref)
        dv_ref[...] = jnp.zeros_like(dv_ref)
        for b in range(NKB):
            kt_ref[b] = k_ref[b * TK : (b + 1) * TK, :].T

    first = step * TQ
    place = first + lax.broadcasted_iota(jnp.int32, (1, TQ), 1)
    begin = jnp.zeros((1, TQ), jnp.int32)
    first_begin = jnp.int32(0)
    end = jnp.int32(0)
    for j in range(NDOC):
        end = end + len_ref[seq, j]
        begin = jnp.where(place >= end, end, begin)
        first_begin = jnp.where(first >= end, end, first_begin)
    place = jnp.concatenate([place] * HEADS, axis=1)
    begin = jnp.concatenate([begin] * HEADS, axis=1)
    low = first_begin // TK
    high = (first + TQ - 1) // TK + 1

    q_rows = jnp.concatenate([qg_ref[:, h * DH : (h + 1) * DH] for h in range(HEADS)], axis=0)
    g_rows = jnp.concatenate(
        [qg_ref[:, QW + h * DH : QW + (h + 1) * DH] for h in range(HEADS)], axis=0
    )
    q_cols = q_rows.T
    g_cols = g_rows.T

    def window(count):
        keys = count * TK
        rows = pl.ds(pl.multiple_of(low * TK, TK), keys)
        s_all = jnp.dot(k_ref[rows, :], q_cols, preferred_element_type=F32)
        dp_all = jnp.dot(v_ref[rows, :], g_cols, preferred_element_type=F32)
        tops, masses, sums = [], [], []
        for r in range(keys // SUB):
            rs = slice(r * SUB, (r + 1) * SUB)
            u = low * TK + r * SUB + lax.broadcasted_iota(jnp.int32, (SUB, width), 0)
            s = s_all[rs] * (SCALE * LOG2E)
            seen = u >= begin
            if (r + 1) * SUB > keys - TQ:
                seen = seen & (u <= place)
            s = jnp.where(seen, s, MASKED).reshape(SUB // 8, 8, width)
            top = jnp.max(s, axis=0)
            e = jnp.exp2(s - top[None])
            dp = dp_all[rs].reshape(SUB // 8, 8, width)
            e_ref[rs] = e.reshape(SUB, width)
            dp_ref[rs] = dp_all[rs]
            tops.append(top)
            masses.append(jnp.sum(e, axis=0))
            sums.append(jnp.sum(e * dp, axis=0))
        peak = functools.reduce(jnp.maximum, tops)
        peak = jnp.max(peak, axis=0, keepdims=True)
        scales = [jnp.exp2(top - peak) for top in tops]
        mass = sum(m * f for m, f in zip(masses, scales))
        weighted = sum(m * f for m, f in zip(sums, scales))
        inverse = 1.0 / jnp.sum(mass, axis=0, keepdims=True)
        delta = jnp.sum(weighted, axis=0, keepdims=True) * inverse
        inverse = jnp.broadcast_to(inverse, (8, width))
        delta = jnp.broadcast_to(delta, (8, width))
        dq = None
        for j in range(count):
            low_probs, ds = [], []
            for r in range(j * TK // SUB, (j + 1) * TK // SUB):
                rs = slice(r * SUB, (r + 1) * SUB)
                p = e_ref[rs].reshape(SUB // 8, 8, width) * (scales[r] * inverse)[None]
                d = p * (dp_ref[rs].reshape(SUB // 8, 8, width) - delta[None])
                low_probs.append(p.reshape(SUB, width).astype(BF16))
                ds.append(d.reshape(SUB, width).astype(BF16))
            low_probs = jnp.concatenate(low_probs, axis=0)
            ds = jnp.concatenate(ds, axis=0)
            rows = pl.ds(pl.multiple_of((low + j) * TK, TK), TK)
            dv_ref[rows, :] += jnp.dot(low_probs, g_rows, preferred_element_type=F32)
            dk_ref[rows, :] += jnp.dot(ds, q_rows, preferred_element_type=F32)
            part = jnp.dot(kt_ref[low + j], ds, preferred_element_type=F32)
            dq = part if dq is None else dq + part
        dq = (dq * SCALE).T.astype(BF16)
        out_rows = pl.ds(pl.multiple_of(first, TQ), TQ)
        for h in range(HEADS):
            out_ref[out_rows, h * DH : (h + 1) * DH] = dq[h * TQ : (h + 1) * TQ]

    for count in range(1, MOST + 1):
        pl.when(high - low == count)(functools.partial(window, count))

    last = step == pl.num_programs(0) - 1

    @pl.when(last)
    def _():
        out_ref[:, QW : QW + DH] = (dk_ref[...] * SCALE).astype(BF16)
        out_ref[:, QW + DH : OUT_W] = dv_ref[...].astype(BF16)


def attention(own, assignment, doc_lengths, rows, other):
    width = HEADS * TQ
    return pl.pallas_call(
        attention_kernel,
        out_shape=jax.ShapeDtypeStruct((LEN, OUT_W), BF16),
        grid_spec=pltpu.PrefetchScalarGridSpec(
            num_scalar_prefetch=3,
            grid=(LEN // TQ,),
            in_specs=[
                pl.BlockSpec((TQ, 2 * QW), lambda i, *_: (i, 0)),
                pl.BlockSpec((LEN, DH), lambda i, *_: (0, 2 * QW // DH)),
                pl.BlockSpec((LEN, DH), lambda i, *_: (0, 0)),
            ],
            out_specs=pl.BlockSpec((LEN, OUT_W), lambda i, *_: (0, 0)),
            scratch_shapes=[
                pltpu.VMEM((LEN, DH), BF16),
                pltpu.VMEM((LEN, DH), BF16),
                pltpu.VMEM((NKB, DH, TK), BF16),
                pltpu.VMEM((MOST * TK, width), F32),
                pltpu.VMEM((MOST * TK, width), F32),
                pltpu.VMEM((LEN, DH), F32),
                pltpu.VMEM((LEN, DH), F32),
            ],
        ),
        compiler_params=pltpu.CompilerParams(vmem_limit_bytes=40 * MIB),
        name="attention",
    )(own, assignment, doc_lengths, rows, rows, other)


def unpack_kernel(in_hbm, dq_hbm, dk_ref, dv_ref, in_ref, dq_ref, in_sem, out_sem):
    pieces = [slice(i * PIECE, (i + 1) * PIECE) for i in range(OWN // PIECE)]
    loads = [pltpu.make_async_copy(in_hbm.at[:, rows], in_ref.at[:, rows], in_sem.at[i]) for i, rows in enumerate(pieces)]
    for move in loads:
        move.start()
    stores = []
    for i, rows in enumerate(pieces):
        loads[i].wait()
        for j in range(HK):
            dk = jnp.zeros((PIECE, DH), F32)
            dv = jnp.zeros((PIECE, DH), F32)
            for p in range(j * SHARE, (j + 1) * SHARE):
                dq_ref[0, rows, p * QW : (p + 1) * QW] = in_ref[p, rows, 0:QW]
                dk = dk + in_ref[p, rows, QW : QW + DH].astype(F32)
                dv = dv + in_ref[p, rows, QW + DH : OUT_W].astype(F32)
            dk_ref[0, rows, j * DH : (j + 1) * DH] = dk.astype(BF16)
            dv_ref[0, rows, j * DH : (j + 1) * DH] = dv.astype(BF16)
        move = pltpu.make_async_copy(dq_ref.at[:, rows], dq_hbm.at[:, rows], out_sem.at[i])
        move.start()
        stores.append(move)
    for move in stores:
        move.wait()


def unpack(blocks):
    return pl.pallas_call(
        unpack_kernel,
        out_shape=(
            jax.ShapeDtypeStruct((1, OWN, HQ * DH), BF16),
            jax.ShapeDtypeStruct((1, OWN, HK * DH), BF16),
            jax.ShapeDtypeStruct((1, OWN, HK * DH), BF16),
        ),
        in_specs=[pl.BlockSpec(memory_space=pl.ANY)],
        out_specs=(
            pl.BlockSpec(memory_space=pl.ANY),
            pl.BlockSpec(memory_space=pltpu.VMEM),
            pl.BlockSpec(memory_space=pltpu.VMEM),
        ),
        scratch_shapes=[
            pltpu.VMEM((CTX, OWN, OUT_W), BF16),
            pltpu.VMEM((1, OWN, HQ * DH), BF16),
            pltpu.SemaphoreType.DMA((OWN // PIECE,)),
            pltpu.SemaphoreType.DMA((OWN // PIECE,)),
        ],
        compiler_params=pltpu.CompilerParams(vmem_limit_bytes=24 * MIB),
        name="unpack",
    )(blocks)


def swap_cores(x):
    return lax.ppermute(x, "ctx", [(i, i ^ 1) for i in range(CTX)])


def local(query_rows, key_rows, value_rows, out_grad, doc_lengths, assignment):
    own = jnp.stack([lax.axis_index("dp"), lax.axis_index("ctx") % CORES]).astype(jnp.int32)
    sent = pack(assignment, query_rows, out_grad, key_rows, value_rows)
    got = lax.all_to_all(sent, ("ctx", "dp"), split_axis=0, concat_axis=0, tiled=True)
    rows = got.reshape(LEN, IN_W)
    other = swap_cores(rows[:, 2 * QW : IN_W])
    grads = attention(own, assignment, doc_lengths, rows, other)
    back = lax.all_to_all(
        grads.reshape(CTX, OWN, OUT_W), "ctx", split_axis=0, concat_axis=0, tiled=True
    )
    return unpack(back)


def solution(mesh):
    placed = (
        P(None, ("ctx", "dp"), None),
        P(None, ("ctx", "dp"), None),
        P(None, ("ctx", "dp"), None),
        P(None, ("ctx", "dp"), None),
        P(),
        P(),
    )
    return jax.shard_map(
        local,
        mesh=mesh,
        in_specs=placed,
        out_specs=(P("dp", "ctx", None), P("dp", "ctx", None), P("dp", "ctx", None)),
        check_vma=False,
    )
```

```python
import functools
import math

import jax
import jax.numpy as jnp
from jax import lax
from jax.experimental import pallas as pl
from jax.experimental.pallas import tpu as pltpu
from jax.sharding import Mesh, PartitionSpec as P

HQ = 32
HK = 4
DH = 128
NDOC = 8
LEN = 2048

Y_HI, Z, CORES, X, Y_LO = 2, 4, 2, 4, 2
CTX_AXES = ("y_hi", "z", "core")
DP_AXES = ("x", "y_lo")
IN_AXES = ("x", "z", "y_hi", "y_lo")
OUT_AXES = ("z", "y_hi")
CTX = Y_HI * Z * CORES
DP = X * Y_LO
CHIPS = Y_HI * Z
ROWS = LEN // (CTX * DP)
OWN = LEN // CTX
HEADS = HQ // CHIPS
QW = HEADS * DH
SHARE = CHIPS // HK
IN_W = 2 * QW + 2 * DH
OUT_W = QW + 2 * DH
PIECE = 32

WIDTH = HEADS * OWN
BLOCKS = LEN // OWN
MOST = (LEN // 2 + OWN - 2) // OWN + 1

SCALE = DH ** (-0.5)
LOG2E = math.log2(math.e)
MASKED = -1e30
F32 = jnp.float32
BF16 = jnp.bfloat16
MIB = 1024 * 1024


def out_slot(chip):
    return chip % Z * Y_HI + chip // Z


def pack_kernel(seq_ref, q_in, g_in, k_in, v_in, out, q_ref, g_ref, k_ref, v_ref, out_ref, in_sem, out_sem):
    wide = SHARE * QW

    def load(j, a, source, held, width):
        cols = slice(j * width, (j + 1) * width)
        return pltpu.make_async_copy(source.at[:, :, cols], held.at[:, :, cols], in_sem.at[j, a])

    loads = [
        [load(j, 0, q_in, q_ref, wide), load(j, 1, g_in, g_ref, wide), load(j, 2, k_in, k_ref, DH), load(j, 3, v_in, v_ref, DH)]
        for j in range(HK)
    ]
    for group in loads:
        for move in group:
            move.start()
    stores = []
    for j in range(HK):
        for move in loads[j]:
            move.wait()
        thin = slice(j * DH, (j + 1) * DH)
        for chip in range(j * SHARE, (j + 1) * SHARE):
            cols = slice(chip * QW, (chip + 1) * QW)
            y_hi, z = chip // Z, chip % Z
            for group in range(DP):
                seq = seq_ref[group]
                x, y_lo = group // Y_LO, group % Y_LO
                out_ref[x, z, y_hi, y_lo, :, 0:QW] = q_ref[seq, :, cols]
                out_ref[x, z, y_hi, y_lo, :, QW : 2 * QW] = g_ref[seq, :, cols]
                out_ref[x, z, y_hi, y_lo, :, 2 * QW : 2 * QW + DH] = k_ref[seq, :, thin]
                out_ref[x, z, y_hi, y_lo, :, 2 * QW + DH : IN_W] = v_ref[seq, :, thin]
            move = pltpu.make_async_copy(out_ref.at[:, z, y_hi], out.at[:, z, y_hi], out_sem.at[chip])
            move.start()
            stores.append(move)
    for move in stores:
        move.wait()


def pack(assignment, query_rows, out_grad, key_rows, value_rows):
    whole = pl.BlockSpec(memory_space=pl.ANY)
    shape = (X, Z, Y_HI, Y_LO, ROWS, IN_W)
    return pl.pallas_call(
        pack_kernel,
        out_shape=jax.ShapeDtypeStruct(shape, BF16),
        in_specs=[pl.BlockSpec(memory_space=pltpu.SMEM)] + [whole] * 4,
        out_specs=whole,
        scratch_shapes=[
            pltpu.VMEM((DP, ROWS, HQ * DH), BF16),
            pltpu.VMEM((DP, ROWS, HQ * DH), BF16),
            pltpu.VMEM((DP, ROWS, HK * DH), BF16),
            pltpu.VMEM((DP, ROWS, HK * DH), BF16),
            pltpu.VMEM(shape, BF16),
            pltpu.SemaphoreType.DMA((HK, 4)),
            pltpu.SemaphoreType.DMA((CHIPS,)),
        ],
        compiler_params=pltpu.CompilerParams(vmem_limit_bytes=60 * MIB),
        name="pack",
    )(assignment, query_rows, out_grad, key_rows, value_rows)


def block_rows(block):
    return pl.ds(pl.multiple_of(block * OWN, OWN), OWN)


def attention_kernel(
    own_ref, seq_ref, len_ref, qg_ref, mine_ref, other_ref, out_ref, give_ref, k_ref, v_ref, kt_ref, e_ref, dp_ref, dk_ref, dv_ref
):
    step = pl.program_id(0)
    seq = seq_ref[own_ref[0]]
    core = own_ref[1]
    block = step * CORES + core

    @pl.when(step == 0)
    def _():
        dk_ref[...] = jnp.zeros_like(dk_ref)
        dv_ref[...] = jnp.zeros_like(dv_ref)
        for chip in range(CHIPS):
            for got_ref, got_core in ((mine_ref, core), (other_ref, 1 - core)):
                got = got_ref[:, chip % Z, chip // Z].reshape(OWN, 2 * DH)
                rows = block_rows(chip * CORES + got_core)
                k_ref[rows, :] = got[:, 0:DH]
                v_ref[rows, :] = got[:, DH : 2 * DH]
                kt_ref[chip * CORES + got_core] = got[:, 0:DH].T

    first = block * OWN
    place = first + lax.broadcasted_iota(jnp.int32, (1, OWN), 1)
    begin = jnp.zeros((1, OWN), jnp.int32)
    first_begin = jnp.int32(0)
    end = jnp.int32(0)
    for j in range(NDOC):
        end = end + len_ref[seq, j]
        begin = jnp.where(place >= end, end, begin)
        first_begin = jnp.where(first >= end, end, first_begin)
    place = jnp.concatenate([place] * HEADS, axis=1)
    begin = jnp.concatenate([begin] * HEADS, axis=1)
    low = first_begin // OWN

    qg = qg_ref[...].reshape(OWN, 2 * QW)
    q_rows = jnp.concatenate([qg[:, h * DH : (h + 1) * DH] for h in range(HEADS)], axis=0)
    g_rows = jnp.concatenate([qg[:, QW + h * DH : QW + (h + 1) * DH] for h in range(HEADS)], axis=0)
    q_cols = q_rows.T
    g_cols = g_rows.T

    def window(count):
        keys = pl.ds(pl.multiple_of(low * OWN, OWN), count * OWN)
        s_all = jnp.dot(k_ref[keys, :], q_cols, preferred_element_type=F32)
        dp_all = jnp.dot(v_ref[keys, :], g_cols, preferred_element_type=F32)
        tops, masses, sums = [], [], []
        for r in range(count):
            rs = slice(r * OWN, (r + 1) * OWN)
            u = (low + r) * OWN + lax.broadcasted_iota(jnp.int32, (OWN, WIDTH), 0)
            seen = u >= begin
            if r == count - 1:
                seen = seen & (u <= place)
            s = jnp.where(seen, s_all[rs] * (SCALE * LOG2E), MASKED).reshape(OWN // 8, 8, WIDTH)
            top = jnp.max(s, axis=0)
            e = jnp.exp2(s - top[None])
            e_ref[rs] = e.reshape(OWN, WIDTH)
            dp_ref[rs] = dp_all[rs]
            tops.append(top)
            masses.append(jnp.sum(e, axis=0))
            sums.append(jnp.sum(e * dp_all[rs].reshape(OWN // 8, 8, WIDTH), axis=0))
        peak = jnp.max(functools.reduce(jnp.maximum, tops), axis=0, keepdims=True)
        scales = [jnp.exp2(top - peak) for top in tops]
        mass = sum(m * f for m, f in zip(masses, scales))
        weighted = sum(m * f for m, f in zip(sums, scales))
        inverse = 1.0 / jnp.sum(mass, axis=0, keepdims=True)
        delta = jnp.sum(weighted, axis=0, keepdims=True) * inverse
        inverse = jnp.broadcast_to(inverse, (8, WIDTH))
        delta = jnp.broadcast_to(delta, (8, WIDTH))
        dq = None
        done = 0
        while done < count:
            size = 2 - (count - done) % 2
            low_probs, ds = [], []
            for r in range(done, done + size):
                rs = slice(r * OWN, (r + 1) * OWN)
                p = e_ref[rs].reshape(OWN // 8, 8, WIDTH) * (scales[r] * inverse)[None]
                d = p * (dp_ref[rs].reshape(OWN // 8, 8, WIDTH) - delta[None])
                low_probs.append(p.reshape(OWN, WIDTH).astype(BF16))
                ds.append(d.reshape(OWN, WIDTH).astype(BF16))
            low_probs = jnp.concatenate(low_probs, axis=0)
            ds = jnp.concatenate(ds, axis=0)
            rows = pl.ds(pl.multiple_of((low + done) * OWN, OWN), size * OWN)
            dv_ref[rows, :] += jnp.dot(low_probs, g_rows, preferred_element_type=F32)
            dk_ref[rows, :] += jnp.dot(ds, q_rows, preferred_element_type=F32)
            kt = jnp.concatenate([kt_ref[low + done + i] for i in range(size)], axis=1)
            part = jnp.dot(kt, ds, preferred_element_type=F32)
            dq = part if dq is None else dq + part
            done += size
        dq = (dq * SCALE).T.astype(BF16)
        for h in range(HEADS):
            out_ref[out_slot(step), :, h * DH : (h + 1) * DH] = dq[h * OWN : (h + 1) * OWN]

    for count in range(1, MOST + 1):
        pl.when(block - low + 1 == count)(functools.partial(window, count))

    @pl.when(step == pl.num_programs(0) - 1)
    def _():
        for chip in range(CHIPS):
            slot = out_slot(chip)
            rows = block_rows(chip * CORES + core)
            out_ref[slot, :, QW : QW + DH] = (dk_ref[rows, :] * SCALE).astype(BF16)
            out_ref[slot, :, QW + DH : OUT_W] = dv_ref[rows, :].astype(BF16)
            rows = block_rows(chip * CORES + 1 - core)
            give_ref[slot, :, 0:DH] = (dk_ref[rows, :] * SCALE).astype(BF16)
            give_ref[slot, :, DH : 2 * DH] = dv_ref[rows, :].astype(BF16)


def attention(own, assignment, doc_lengths, rows, other):
    held = (X, Z, Y_HI, Y_LO * ROWS, 2 * DH)
    return pl.pallas_call(
        attention_kernel,
        out_shape=(
            jax.ShapeDtypeStruct((CHIPS, OWN, OUT_W), BF16),
            jax.ShapeDtypeStruct((CHIPS, OWN, 2 * DH), BF16),
        ),
        grid_spec=pltpu.PrefetchScalarGridSpec(
            num_scalar_prefetch=3,
            grid=(CHIPS,),
            in_specs=[
                pl.BlockSpec((X, 1, 1, Y_LO * ROWS, 2 * QW), lambda i, *_: (0, i % Z, i // Z, 0, 0)),
                pl.BlockSpec(held, lambda i, *_: (0, 0, 0, 0, QW // DH)),
                pl.BlockSpec(held, lambda i, *_: (0, 0, 0, 0, 0)),
            ],
            out_specs=(
                pl.BlockSpec((CHIPS, OWN, OUT_W), lambda i, *_: (0, 0, 0)),
                pl.BlockSpec((CHIPS, OWN, 2 * DH), lambda i, *_: (0, 0, 0)),
            ),
            scratch_shapes=[
                pltpu.VMEM((LEN, DH), BF16),
                pltpu.VMEM((LEN, DH), BF16),
                pltpu.VMEM((BLOCKS, DH, OWN), BF16),
                pltpu.VMEM((MOST * OWN, WIDTH), F32),
                pltpu.VMEM((MOST * OWN, WIDTH), F32),
                pltpu.VMEM((LEN, DH), F32),
                pltpu.VMEM((LEN, DH), F32),
            ],
        ),
        compiler_params=pltpu.CompilerParams(vmem_limit_bytes=40 * MIB),
        name="attention",
    )(own, assignment, doc_lengths, rows, rows, other)


def add_kernel(a_ref, b_ref, out_ref):
    out_ref[...] = (a_ref[...].astype(F32) + b_ref[...].astype(F32)).astype(BF16)


def add_partials(grads, given):
    some = CHIPS // 4
    tail = pl.BlockSpec((some, OWN, 2 * DH), lambda i: (i, 0, QW // (2 * DH)))
    return pl.pallas_call(
        add_kernel,
        out_shape=jax.ShapeDtypeStruct(grads.shape, BF16),
        grid=(CHIPS // some,),
        in_specs=[tail, pl.BlockSpec((some, OWN, 2 * DH), lambda i: (i, 0, 0))],
        out_specs=tail,
        input_output_aliases={0: 0},
        compiler_params=pltpu.CompilerParams(vmem_limit_bytes=8 * MIB),
        name="add_partials",
    )(grads, given)


def unpack_kernel(in_hbm, dq_hbm, dk_ref, dv_ref, in_ref, dq_ref, in_sem, out_sem):
    pieces = [slice(i * PIECE, (i + 1) * PIECE) for i in range(OWN // PIECE)]
    loads = [pltpu.make_async_copy(in_hbm.at[:, rows], in_ref.at[:, rows], in_sem.at[i]) for i, rows in enumerate(pieces)]
    for move in loads:
        move.start()
    stores = []
    for i, rows in enumerate(pieces):
        loads[i].wait()
        for j in range(HK):
            dk = jnp.zeros((PIECE, DH), F32)
            dv = jnp.zeros((PIECE, DH), F32)
            for chip in range(j * SHARE, (j + 1) * SHARE):
                slot = out_slot(chip)
                dq_ref[0, rows, chip * QW : (chip + 1) * QW] = in_ref[slot, rows, 0:QW]
                dk = dk + in_ref[slot, rows, QW : QW + DH].astype(F32)
                dv = dv + in_ref[slot, rows, QW + DH : OUT_W].astype(F32)
            dk_ref[0, rows, j * DH : (j + 1) * DH] = dk.astype(BF16)
            dv_ref[0, rows, j * DH : (j + 1) * DH] = dv.astype(BF16)
        move = pltpu.make_async_copy(dq_ref.at[:, rows], dq_hbm.at[:, rows], out_sem.at[i])
        move.start()
        stores.append(move)
    for move in stores:
        move.wait()


def unpack(blocks):
    return pl.pallas_call(
        unpack_kernel,
        out_shape=(
            jax.ShapeDtypeStruct((1, OWN, HQ * DH), BF16),
            jax.ShapeDtypeStruct((1, OWN, HK * DH), BF16),
            jax.ShapeDtypeStruct((1, OWN, HK * DH), BF16),
        ),
        in_specs=[pl.BlockSpec(memory_space=pl.ANY)],
        out_specs=(
            pl.BlockSpec(memory_space=pl.ANY),
            pl.BlockSpec(memory_space=pltpu.VMEM),
            pl.BlockSpec(memory_space=pltpu.VMEM),
        ),
        scratch_shapes=[
            pltpu.VMEM((CHIPS, OWN, OUT_W), BF16),
            pltpu.VMEM((1, OWN, HQ * DH), BF16),
            pltpu.SemaphoreType.DMA((OWN // PIECE,)),
            pltpu.SemaphoreType.DMA((OWN // PIECE,)),
        ],
        compiler_params=pltpu.CompilerParams(vmem_limit_bytes=24 * MIB),
        name="unpack",
    )(blocks)


def swap_cores(x):
    return lax.ppermute(x, "core", [(0, 1), (1, 0)])


def local(query_rows, key_rows, value_rows, out_grad, doc_lengths, assignment):
    own = jnp.stack([lax.axis_index(DP_AXES), lax.axis_index("core")]).astype(jnp.int32)
    sent = pack(assignment, query_rows, out_grad, key_rows, value_rows).reshape(CHIPS * DP, ROWS, IN_W)
    got = lax.all_to_all(sent, IN_AXES, split_axis=0, concat_axis=0, tiled=True)
    rows = got.reshape(X, Z, Y_HI, Y_LO * ROWS, IN_W)
    other = swap_cores(rows[..., 2 * QW : IN_W])
    grads, give = attention(own, assignment, doc_lengths, rows, other)
    grads = add_partials(grads, swap_cores(give))
    back = lax.all_to_all(grads, OUT_AXES, split_axis=0, concat_axis=0, tiled=True)
    return unpack(back)


def solution(mesh):
    fine = Mesh(mesh.devices.reshape(Y_HI, Z, CORES, X, Y_LO), CTX_AXES + DP_AXES)
    placed = P(None, CTX_AXES + DP_AXES, None)
    return jax.shard_map(
        local,
        mesh=fine,
        in_specs=(placed, placed, placed, placed, P(), P()),
        out_specs=(P(DP_AXES, CTX_AXES, None),) * 3,
        check_vma=False,
    )
```

```python
import functools
import math

import jax
import jax.numpy as jnp
from jax import lax
from jax.experimental import pallas as pl
from jax.experimental.pallas import tpu as pltpu
from jax.sharding import Mesh, PartitionSpec as P

HQ = 32
HK = 4
DH = 128
NDOC = 8
LEN = 2048

Y_HI, Z, CORES, X, Y_LO = 2, 4, 2, 4, 2
CTX_AXES = ("y_hi", "z", "core")
DP_AXES = ("x", "y_lo")
IN_AXES = ("x", "z", "y_hi", "y_lo")
OUT_AXES = ("z", "y_hi")
CTX = Y_HI * Z * CORES
DP = X * Y_LO
CHIPS = Y_HI * Z
ROWS = LEN // (CTX * DP)
OWN = LEN // CTX
HEADS = HQ // CHIPS
QW = HEADS * DH
SHARE = CHIPS // HK
IN_W = 2 * QW + 2 * DH
OUT_W = QW + 2 * DH
PIECE = 32
UNROLL = 8

WIDTH = HEADS * OWN
BLOCKS = LEN // OWN
MOST = (LEN // 2 + OWN - 2) // OWN + 1

SCALE = DH ** (-0.5)
LOG2E = math.log2(math.e)
MASKED = -1e30
F32 = jnp.float32
BF16 = jnp.bfloat16
MIB = 1024 * 1024


def out_slot(chip):
    return chip % Z * Y_HI + chip // Z


def pack_kernel(seq_ref, q_in, g_in, k_in, v_in, out, q_ref, g_ref, k_ref, v_ref, out_ref, in_sem, out_sem):
    wide = SHARE * QW

    def load(j, a, source, held, width):
        cols = slice(j * width, (j + 1) * width)
        return pltpu.make_async_copy(source.at[:, :, cols], held.at[:, :, cols], in_sem.at[j, a])

    loads = [
        [load(j, 0, q_in, q_ref, wide), load(j, 1, g_in, g_ref, wide), load(j, 2, k_in, k_ref, DH), load(j, 3, v_in, v_ref, DH)]
        for j in range(HK)
    ]
    for group in loads:
        for move in group:
            move.start()
    stores = []
    for j in range(HK):
        for move in loads[j]:
            move.wait()
        thin = slice(j * DH, (j + 1) * DH)
        for chip in range(j * SHARE, (j + 1) * SHARE):
            cols = slice(chip * QW, (chip + 1) * QW)
            y_hi, z = chip // Z, chip % Z
            for group in range(DP):
                seq = seq_ref[group]
                x, y_lo = group // Y_LO, group % Y_LO
                out_ref[x, z, y_hi, y_lo, :, 0:QW] = q_ref[seq, :, cols]
                out_ref[x, z, y_hi, y_lo, :, QW : 2 * QW] = g_ref[seq, :, cols]
                out_ref[x, z, y_hi, y_lo, :, 2 * QW : 2 * QW + DH] = k_ref[seq, :, thin]
                out_ref[x, z, y_hi, y_lo, :, 2 * QW + DH : IN_W] = v_ref[seq, :, thin]
            move = pltpu.make_async_copy(out_ref.at[:, z, y_hi], out.at[:, z, y_hi], out_sem.at[chip])
            move.start()
            stores.append(move)
    for move in stores:
        move.wait()


def pack(assignment, query_rows, out_grad, key_rows, value_rows):
    whole = pl.BlockSpec(memory_space=pl.ANY)
    shape = (X, Z, Y_HI, Y_LO, ROWS, IN_W)
    return pl.pallas_call(
        pack_kernel,
        out_shape=jax.ShapeDtypeStruct(shape, BF16),
        in_specs=[pl.BlockSpec(memory_space=pltpu.SMEM)] + [whole] * 4,
        out_specs=whole,
        scratch_shapes=[
            pltpu.VMEM((DP, ROWS, HQ * DH), BF16),
            pltpu.VMEM((DP, ROWS, HQ * DH), BF16),
            pltpu.VMEM((DP, ROWS, HK * DH), BF16),
            pltpu.VMEM((DP, ROWS, HK * DH), BF16),
            pltpu.VMEM(shape, BF16),
            pltpu.SemaphoreType.DMA((HK, 4)),
            pltpu.SemaphoreType.DMA((CHIPS,)),
        ],
        compiler_params=pltpu.CompilerParams(vmem_limit_bytes=60 * MIB),
        name="pack",
    )(assignment, query_rows, out_grad, key_rows, value_rows)


def block_rows(block):
    return pl.ds(pl.multiple_of(block * OWN, OWN), OWN)


def documents(block, seq, len_ref):
    first = block * OWN
    place = first + lax.broadcasted_iota(jnp.int32, (1, OWN), 1)
    begin = jnp.zeros((1, OWN), jnp.int32)
    first_begin = jnp.int32(0)
    end = jnp.int32(0)
    for j in range(NDOC):
        end = end + len_ref[seq, j]
        begin = jnp.where(place >= end, end, begin)
        first_begin = jnp.where(first >= end, end, first_begin)
    place = jnp.concatenate([place] * HEADS, axis=1)
    begin = jnp.concatenate([begin] * HEADS, axis=1)
    return place, begin, first_begin


def queries(step, got_ref):
    qg = got_ref[:, step % Z, step // Z, :, 0 : 2 * QW].reshape(OWN, 2 * QW)
    q_rows = jnp.concatenate([qg[:, h * DH : (h + 1) * DH] for h in range(HEADS)], axis=0)
    g_rows = jnp.concatenate([qg[:, QW + h * DH : QW + (h + 1) * DH] for h in range(HEADS)], axis=0)
    q_cols = q_rows.T
    g_cols = g_rows.T
    return q_rows, g_rows, q_cols, g_cols


def weigh(s, dp, seen):
    s = jnp.where(seen, s * (SCALE * LOG2E), MASKED).reshape(OWN // 8, 8, WIDTH)
    top = jnp.max(s, axis=0)
    e = jnp.exp2(s - top[None])
    return e.reshape(OWN, WIDTH), top, jnp.sum(e, axis=0), jnp.sum(e * dp.reshape(OWN // 8, 8, WIDTH), axis=0)


def key_places(block):
    return block * OWN + lax.broadcasted_iota(jnp.int32, (OWN, WIDTH), 0)


def diagonal_kernel(own_ref, seq_ref, len_ref, got_ref, e_ref, dp_ref, stat_ref):
    seq = seq_ref[own_ref[0]]
    core = own_ref[1]

    def one_block(step, _):
        block = step * CORES + core
        place, begin, _first = documents(block, seq, len_ref)
        _q, _g, q_cols, g_cols = queries(step, got_ref)
        kv = got_ref[:, step % Z, step // Z, :, 2 * QW : IN_W].reshape(OWN, 2 * DH)
        s = jnp.dot(kv[:, 0:DH], q_cols, preferred_element_type=F32)
        dp = jnp.dot(kv[:, DH : 2 * DH], g_cols, preferred_element_type=F32)
        u = key_places(block)
        e, top, mass, weighted = weigh(s, dp, (u >= begin) & (u <= place))
        e_ref[step] = e
        dp_ref[step] = dp
        stat_ref[step, 0] = top
        stat_ref[step, 1] = mass
        stat_ref[step, 2] = weighted
        return 0

    lax.fori_loop(0, CHIPS, one_block, 0, unroll=UNROLL)


def diagonal(own, assignment, doc_lengths, rows):
    small = pl.BlockSpec(memory_space=pltpu.SMEM)
    large = pl.BlockSpec(memory_space=pltpu.VMEM)
    return pl.pallas_call(
        diagonal_kernel,
        out_shape=(
            jax.ShapeDtypeStruct((CHIPS, OWN, WIDTH), F32),
            jax.ShapeDtypeStruct((CHIPS, OWN, WIDTH), F32),
            jax.ShapeDtypeStruct((CHIPS, 3, 8, WIDTH), F32),
        ),
        in_specs=[small, small, small, large],
        out_specs=(large, large, large),
        compiler_params=pltpu.CompilerParams(vmem_limit_bytes=24 * MIB),
        cost_estimate=pl.CostEstimate(
            flops=4 * CHIPS * OWN * WIDTH * DH, bytes_accessed=8 * MIB, transcendentals=CHIPS * OWN * WIDTH
        ),
        name="diagonal",
    )(own, assignment, doc_lengths, rows)


def attention_kernel(
    own_ref, seq_ref, len_ref, got_ref, other_ref, diag_e_ref, diag_dp_ref, diag_stat_ref, out_ref, give_ref, k_ref, v_ref, kt_ref, e_ref, dp_ref, dk_ref, dv_ref
):
    seq = seq_ref[own_ref[0]]
    core = own_ref[1]
    dk_ref[...] = jnp.zeros_like(dk_ref)
    dv_ref[...] = jnp.zeros_like(dv_ref)
    for chip in range(CHIPS):
        place = (slice(None), chip % Z, chip // Z)
        mine = got_ref[(*place, slice(None), slice(2 * QW, IN_W))]
        for got, got_core in ((mine, core), (other_ref[place], 1 - core)):
            got = got.reshape(OWN, 2 * DH)
            rows = block_rows(chip * CORES + got_core)
            k_ref[rows, :] = got[:, 0:DH]
            v_ref[rows, :] = got[:, DH : 2 * DH]
            kt_ref[chip * CORES + got_core] = got[:, 0:DH].T

    def one_block(step, _):
        query_block(step, core, seq, len_ref, got_ref, diag_e_ref, diag_dp_ref, diag_stat_ref, out_ref, k_ref, v_ref, kt_ref, e_ref, dp_ref, dk_ref, dv_ref)
        return _

    lax.fori_loop(0, CHIPS, one_block, 0)
    for chip in range(CHIPS):
        slot = out_slot(chip)
        rows = block_rows(chip * CORES + core)
        out_ref[slot, :, QW : QW + DH] = (dk_ref[rows, :] * SCALE).astype(BF16)
        out_ref[slot, :, QW + DH : OUT_W] = dv_ref[rows, :].astype(BF16)
        rows = block_rows(chip * CORES + 1 - core)
        give_ref[slot, :, 0:DH] = (dk_ref[rows, :] * SCALE).astype(BF16)
        give_ref[slot, :, DH : 2 * DH] = dv_ref[rows, :].astype(BF16)


def query_block(step, core, seq, len_ref, got_ref, diag_e_ref, diag_dp_ref, diag_stat_ref, out_ref, k_ref, v_ref, kt_ref, e_ref, dp_ref, dk_ref, dv_ref):
    block = step * CORES + core
    place, begin, first_begin = documents(block, seq, len_ref)
    low = first_begin // OWN

    q_rows, g_rows, q_cols, g_cols = queries(step, got_ref)

    def window(count):
        tops, masses, sums = [], [], []
        if count > 1:
            keys = pl.ds(pl.multiple_of(low * OWN, OWN), (count - 1) * OWN)
            s_all = jnp.dot(k_ref[keys, :], q_cols, preferred_element_type=F32)
            dp_all = jnp.dot(v_ref[keys, :], g_cols, preferred_element_type=F32)
        for r in range(count - 1):
            rs = slice(r * OWN, (r + 1) * OWN)
            e, top, mass, weighted = weigh(s_all[rs], dp_all[rs], key_places(low + r) >= begin)
            e_ref[rs] = e
            dp_ref[rs] = dp_all[rs]
            tops.append(top)
            masses.append(mass)
            sums.append(weighted)
        tops.append(diag_stat_ref[step, 0])
        masses.append(diag_stat_ref[step, 1])
        sums.append(diag_stat_ref[step, 2])

        def kept(ref, diag_ref, r):
            held = diag_ref[step] if r == count - 1 else ref[r * OWN : (r + 1) * OWN]
            return held.reshape(OWN // 8, 8, WIDTH)

        peak = jnp.max(functools.reduce(jnp.maximum, tops), axis=0, keepdims=True)
        scales = [jnp.exp2(top - peak) for top in tops]
        mass = sum(m * f for m, f in zip(masses, scales))
        weighted = sum(m * f for m, f in zip(sums, scales))
        inverse = 1.0 / jnp.sum(mass, axis=0, keepdims=True)
        delta = jnp.sum(weighted, axis=0, keepdims=True) * inverse
        inverse = jnp.broadcast_to(inverse, (8, WIDTH))
        delta = jnp.broadcast_to(delta, (8, WIDTH))
        dq = None
        done = 0
        while done < count:
            size = (count - done) % 4 or 4
            low_probs, ds = [], []
            for r in range(done, done + size):
                p = kept(e_ref, diag_e_ref, r) * (scales[r] * inverse)[None]
                d = p * (kept(dp_ref, diag_dp_ref, r) - delta[None])
                low_probs.append(p.reshape(OWN, WIDTH).astype(BF16))
                ds.append(d.reshape(OWN, WIDTH).astype(BF16))
            low_probs = jnp.concatenate(low_probs, axis=0)
            ds = jnp.concatenate(ds, axis=0)
            rows = pl.ds(pl.multiple_of((low + done) * OWN, OWN), size * OWN)
            dv_ref[rows, :] += jnp.dot(low_probs, g_rows, preferred_element_type=F32)
            dk_ref[rows, :] += jnp.dot(ds, q_rows, preferred_element_type=F32)
            kt = jnp.concatenate([kt_ref[low + done + i] for i in range(size)], axis=1)
            part = jnp.dot(kt, ds, preferred_element_type=F32)
            dq = part if dq is None else dq + part
            done += size
        dq = (dq * SCALE).astype(BF16).T
        for h in range(HEADS):
            out_ref[out_slot(step), :, h * DH : (h + 1) * DH] = dq[h * OWN : (h + 1) * OWN]

    for count in range(1, MOST + 1):
        pl.when(block - low + 1 == count)(functools.partial(window, count))

def attention(own, assignment, doc_lengths, rows, other, diag):
    small = pl.BlockSpec(memory_space=pltpu.SMEM)
    large = pl.BlockSpec(memory_space=pltpu.VMEM)
    return pl.pallas_call(
        attention_kernel,
        out_shape=(
            jax.ShapeDtypeStruct((CHIPS, OWN, OUT_W), BF16),
            jax.ShapeDtypeStruct((CHIPS, OWN, 2 * DH), BF16),
        ),
        in_specs=[small, small, small] + [large] * 5,
        out_specs=(large, large),
        scratch_shapes=[
            pltpu.VMEM((LEN, DH), BF16),
            pltpu.VMEM((LEN, DH), BF16),
            pltpu.VMEM((BLOCKS, DH, OWN), BF16),
            pltpu.VMEM(((MOST - 1) * OWN, WIDTH), F32),
            pltpu.VMEM(((MOST - 1) * OWN, WIDTH), F32),
            pltpu.VMEM((LEN, DH), F32),
            pltpu.VMEM((LEN, DH), F32),
        ],
        compiler_params=pltpu.CompilerParams(vmem_limit_bytes=40 * MIB),
        name="attention",
    )(own, assignment, doc_lengths, rows, other, *diag)


def add_kernel(a_ref, b_ref, out_ref):
    out_ref[...] = (a_ref[...].astype(F32) + b_ref[...].astype(F32)).astype(BF16)


def add_partials(grads, given):
    some = CHIPS // 4
    tail = pl.BlockSpec((some, OWN, 2 * DH), lambda i: (i, 0, QW // (2 * DH)))
    return pl.pallas_call(
        add_kernel,
        out_shape=jax.ShapeDtypeStruct(grads.shape, BF16),
        grid=(CHIPS // some,),
        in_specs=[tail, pl.BlockSpec((some, OWN, 2 * DH), lambda i: (i, 0, 0))],
        out_specs=tail,
        input_output_aliases={0: 0},
        compiler_params=pltpu.CompilerParams(vmem_limit_bytes=8 * MIB),
        name="add_partials",
    )(grads, given)


def unpack_kernel(in_hbm, dq_hbm, dk_ref, dv_ref, in_ref, dq_ref, in_sem, out_sem):
    pieces = [slice(i * PIECE, (i + 1) * PIECE) for i in range(OWN // PIECE)]
    loads = [pltpu.make_async_copy(in_hbm.at[:, rows], in_ref.at[:, rows], in_sem.at[i]) for i, rows in enumerate(pieces)]
    for move in loads:
        move.start()
    stores = []
    for i, rows in enumerate(pieces):
        loads[i].wait()
        for j in range(HK):
            dk = jnp.zeros((PIECE, DH), F32)
            dv = jnp.zeros((PIECE, DH), F32)
            for chip in range(j * SHARE, (j + 1) * SHARE):
                slot = out_slot(chip)
                dq_ref[0, rows, chip * QW : (chip + 1) * QW] = in_ref[slot, rows, 0:QW]
                dk = dk + in_ref[slot, rows, QW : QW + DH].astype(F32)
                dv = dv + in_ref[slot, rows, QW + DH : OUT_W].astype(F32)
            dk_ref[0, rows, j * DH : (j + 1) * DH] = dk.astype(BF16)
            dv_ref[0, rows, j * DH : (j + 1) * DH] = dv.astype(BF16)
        move = pltpu.make_async_copy(dq_ref.at[:, rows], dq_hbm.at[:, rows], out_sem.at[i])
        move.start()
        stores.append(move)
    for move in stores:
        move.wait()


def unpack(blocks):
    return pl.pallas_call(
        unpack_kernel,
        out_shape=(
            jax.ShapeDtypeStruct((1, OWN, HQ * DH), BF16),
            jax.ShapeDtypeStruct((1, OWN, HK * DH), BF16),
            jax.ShapeDtypeStruct((1, OWN, HK * DH), BF16),
        ),
        in_specs=[pl.BlockSpec(memory_space=pl.ANY)],
        out_specs=(
            pl.BlockSpec(memory_space=pl.ANY),
            pl.BlockSpec(memory_space=pltpu.VMEM),
            pl.BlockSpec(memory_space=pltpu.VMEM),
        ),
        scratch_shapes=[
            pltpu.VMEM((CHIPS, OWN, OUT_W), BF16),
            pltpu.VMEM((1, OWN, HQ * DH), BF16),
            pltpu.SemaphoreType.DMA((OWN // PIECE,)),
            pltpu.SemaphoreType.DMA((OWN // PIECE,)),
        ],
        compiler_params=pltpu.CompilerParams(vmem_limit_bytes=24 * MIB),
        name="unpack",
    )(blocks)


def swap_cores(x):
    return lax.ppermute(x, "core", [(0, 1), (1, 0)])


def local(query_rows, key_rows, value_rows, out_grad, doc_lengths, assignment):
    own = jnp.stack([lax.axis_index(DP_AXES), lax.axis_index("core")]).astype(jnp.int32)
    sent = pack(assignment, query_rows, out_grad, key_rows, value_rows).reshape(CHIPS * DP, ROWS, IN_W)
    got = lax.all_to_all(sent, IN_AXES, split_axis=0, concat_axis=0, tiled=True)
    rows = got.reshape(X, Z, Y_HI, Y_LO * ROWS, IN_W)
    other = swap_cores(rows[..., 2 * QW : IN_W])
    diag = diagonal(own, assignment, doc_lengths, rows)
    grads, give = attention(own, assignment, doc_lengths, rows, other, diag)
    grads = add_partials(grads, swap_cores(give))
    back = lax.all_to_all(grads, OUT_AXES, split_axis=0, concat_axis=0, tiled=True)
    return unpack(back)


def solution(mesh):
    fine = Mesh(mesh.devices.reshape(Y_HI, Z, CORES, X, Y_LO), CTX_AXES + DP_AXES)
    placed = P(None, CTX_AXES + DP_AXES, None)
    return jax.shard_map(
        local,
        mesh=fine,
        in_specs=(placed, placed, placed, placed, P(), P()),
        out_specs=(P(DP_AXES, CTX_AXES, None),) * 3,
        check_vma=False,
    )
```

```python
import functools
import math

import jax
import jax.numpy as jnp
from jax import lax
from jax.experimental import pallas as pl
from jax.experimental.pallas import tpu as pltpu
from jax.sharding import Mesh, PartitionSpec as P

HQ = 32
HK = 4
DH = 128
NDOC = 8
LEN = 2048

Y_HI, Z, CORES, X, Y_LO = 2, 4, 2, 4, 2
CTX_AXES = ("y_hi", "z", "core")
DP_AXES = ("x", "y_lo")
IN_AXES = ("x", "z", "y_hi", "y_lo")
OUT_AXES = ("z", "y_hi")
CTX = Y_HI * Z * CORES
DP = X * Y_LO
CHIPS = Y_HI * Z
ROWS = LEN // (CTX * DP)
OWN = LEN // CTX
HEADS = HQ // CHIPS
QW = HEADS * DH
SHARE = CHIPS // HK
IN_W = 2 * QW + 2 * DH
OUT_W = QW + 2 * DH
PIECE = 32
UNROLL = 8

WIDTH = HEADS * OWN
BLOCKS = LEN // OWN
MOST = (LEN // 2 + OWN - 2) // OWN + 1

SCALE = DH ** (-0.5)
LOG2E = math.log2(math.e)
MASKED = -1e30
F32 = jnp.float32
BF16 = jnp.bfloat16
MIB = 1024 * 1024


def out_slot(chip):
    return chip % Z * Y_HI + chip // Z


def pack_kernel(seq_ref, q_in, g_in, k_in, v_in, out, q_ref, g_ref, k_ref, v_ref, out_ref, in_sem, out_sem):
    wide = SHARE * QW

    def load(j, a, source, held, width):
        cols = slice(j * width, (j + 1) * width)
        return pltpu.make_async_copy(source.at[:, :, cols], held.at[:, :, cols], in_sem.at[j, a])

    loads = [
        [load(j, 0, q_in, q_ref, wide), load(j, 1, g_in, g_ref, wide), load(j, 2, k_in, k_ref, DH), load(j, 3, v_in, v_ref, DH)]
        for j in range(HK)
    ]
    for group in loads:
        for move in group:
            move.start()
    stores = []
    for j in range(HK):
        for move in loads[j]:
            move.wait()
        thin = slice(j * DH, (j + 1) * DH)
        for chip in range(j * SHARE, (j + 1) * SHARE):
            cols = slice(chip * QW, (chip + 1) * QW)
            y_hi, z = chip // Z, chip % Z
            for group in range(DP):
                seq = seq_ref[group]
                x, y_lo = group // Y_LO, group % Y_LO
                out_ref[x, z, y_hi, y_lo, :, 0:QW] = q_ref[seq, :, cols]
                out_ref[x, z, y_hi, y_lo, :, QW : 2 * QW] = g_ref[seq, :, cols]
                out_ref[x, z, y_hi, y_lo, :, 2 * QW : 2 * QW + DH] = k_ref[seq, :, thin]
                out_ref[x, z, y_hi, y_lo, :, 2 * QW + DH : IN_W] = v_ref[seq, :, thin]
            move = pltpu.make_async_copy(out_ref.at[:, z, y_hi], out.at[:, z, y_hi], out_sem.at[chip])
            move.start()
            stores.append(move)
    for move in stores:
        move.wait()


def pack(assignment, query_rows, out_grad, key_rows, value_rows):
    whole = pl.BlockSpec(memory_space=pl.ANY)
    shape = (X, Z, Y_HI, Y_LO, ROWS, IN_W)
    return pl.pallas_call(
        pack_kernel,
        out_shape=jax.ShapeDtypeStruct(shape, BF16),
        in_specs=[pl.BlockSpec(memory_space=pltpu.SMEM)] + [whole] * 4,
        out_specs=whole,
        scratch_shapes=[
            pltpu.VMEM((DP, ROWS, HQ * DH), BF16),
            pltpu.VMEM((DP, ROWS, HQ * DH), BF16),
            pltpu.VMEM((DP, ROWS, HK * DH), BF16),
            pltpu.VMEM((DP, ROWS, HK * DH), BF16),
            pltpu.VMEM(shape, BF16),
            pltpu.SemaphoreType.DMA((HK, 4)),
            pltpu.SemaphoreType.DMA((CHIPS,)),
        ],
        compiler_params=pltpu.CompilerParams(vmem_limit_bytes=60 * MIB),
        name="pack",
    )(assignment, query_rows, out_grad, key_rows, value_rows)


def block_rows(block):
    return pl.ds(pl.multiple_of(block * OWN, OWN), OWN)


def documents(block, seq, len_ref):
    first = block * OWN
    place = first + lax.broadcasted_iota(jnp.int32, (1, OWN), 1)
    begin = jnp.zeros((1, OWN), jnp.int32)
    first_begin = jnp.int32(0)
    end = jnp.int32(0)
    for j in range(NDOC):
        end = end + len_ref[seq, j]
        begin = jnp.where(place >= end, end, begin)
        first_begin = jnp.where(first >= end, end, first_begin)
    place = jnp.concatenate([place] * HEADS, axis=1)
    begin = jnp.concatenate([begin] * HEADS, axis=1)
    return place, begin, first_begin


def queries(step, got_ref):
    qg = got_ref[:, step % Z, step // Z, :, 0 : 2 * QW].reshape(OWN, 2 * QW)
    q_rows = jnp.concatenate([qg[:, h * DH : (h + 1) * DH] for h in range(HEADS)], axis=0)
    g_rows = jnp.concatenate([qg[:, QW + h * DH : QW + (h + 1) * DH] for h in range(HEADS)], axis=0)
    q_cols = q_rows.T
    g_cols = g_rows.T
    return q_rows, g_rows, q_cols, g_cols


def weigh(s, dp, seen):
    s = jnp.where(seen, s * (SCALE * LOG2E), MASKED).reshape(OWN // 8, 8, WIDTH)
    top = jnp.max(s, axis=0)
    e = jnp.exp2(s - top[None])
    return e.reshape(OWN, WIDTH), top, jnp.sum(e, axis=0), jnp.sum(e * dp.reshape(OWN // 8, 8, WIDTH), axis=0)


def key_places(block):
    return block * OWN + lax.broadcasted_iota(jnp.int32, (OWN, WIDTH), 0)


def diagonal_kernel(own_ref, seq_ref, len_ref, got_ref, e_ref, dp_ref, stat_ref):
    seq = seq_ref[own_ref[0]]
    core = own_ref[1]

    def one_block(step, _):
        block = step * CORES + core
        place, begin, _first = documents(block, seq, len_ref)
        _q, _g, q_cols, g_cols = queries(step, got_ref)
        kv = got_ref[:, step % Z, step // Z, :, 2 * QW : IN_W].reshape(OWN, 2 * DH)
        s = jnp.dot(kv[:, 0:DH], q_cols, preferred_element_type=F32)
        dp = jnp.dot(kv[:, DH : 2 * DH], g_cols, preferred_element_type=F32)
        u = key_places(block)
        e, top, mass, weighted = weigh(s, dp, (u >= begin) & (u <= place))
        e_ref[step] = e
        dp_ref[step] = dp
        stat_ref[step, 0] = top
        stat_ref[step, 1] = mass
        stat_ref[step, 2] = weighted
        return 0

    lax.fori_loop(0, CHIPS, one_block, 0, unroll=UNROLL)


def diagonal(own, assignment, doc_lengths, rows):
    small = pl.BlockSpec(memory_space=pltpu.SMEM)
    large = pl.BlockSpec(memory_space=pltpu.VMEM)
    return pl.pallas_call(
        diagonal_kernel,
        out_shape=(
            jax.ShapeDtypeStruct((CHIPS, OWN, WIDTH), F32),
            jax.ShapeDtypeStruct((CHIPS, OWN, WIDTH), F32),
            jax.ShapeDtypeStruct((CHIPS, 3, 8, WIDTH), F32),
        ),
        in_specs=[small, small, small, large],
        out_specs=(large, large, large),
        compiler_params=pltpu.CompilerParams(vmem_limit_bytes=24 * MIB),
        cost_estimate=pl.CostEstimate(
            flops=4 * CHIPS * OWN * WIDTH * DH, bytes_accessed=8 * MIB, transcendentals=CHIPS * OWN * WIDTH
        ),
        name="diagonal",
    )(own, assignment, doc_lengths, rows)


def attention_kernel(
    own_ref, seq_ref, len_ref, got_ref, other_ref, diag_e_ref, diag_dp_ref, diag_stat_ref, out_ref, give_ref, k_ref, v_ref, kt_ref, e_ref, dp_ref, dk_ref, dv_ref
):
    seq = seq_ref[own_ref[0]]
    core = own_ref[1]
    dk_ref[...] = jnp.zeros_like(dk_ref)
    dv_ref[...] = jnp.zeros_like(dv_ref)
    for chip in range(CHIPS):
        place = (slice(None), chip % Z, chip // Z)
        mine = got_ref[(*place, slice(None), slice(2 * QW, IN_W))]
        for got, got_core in ((mine, core), (other_ref[place], 1 - core)):
            got = got.reshape(OWN, 2 * DH)
            rows = block_rows(chip * CORES + got_core)
            k_ref[rows, :] = got[:, 0:DH]
            v_ref[rows, :] = got[:, DH : 2 * DH]
            kt_ref[chip * CORES + got_core] = got[:, 0:DH].T

    def one_block(step, _):
        query_block(step, core, seq, len_ref, got_ref, diag_e_ref, diag_dp_ref, diag_stat_ref, out_ref, k_ref, v_ref, kt_ref, e_ref, dp_ref, dk_ref, dv_ref)
        return _

    lax.fori_loop(0, CHIPS, one_block, 0)
    for chip in range(CHIPS):
        slot = out_slot(chip)
        rows = block_rows(chip * CORES + core)
        out_ref[slot, :, QW : QW + DH] = (dk_ref[rows, :] * SCALE).astype(BF16)
        out_ref[slot, :, QW + DH : OUT_W] = dv_ref[rows, :].astype(BF16)
        rows = block_rows(chip * CORES + 1 - core)
        give_ref[slot, :, 0:DH] = (dk_ref[rows, :] * SCALE).astype(BF16)
        give_ref[slot, :, DH : 2 * DH] = dv_ref[rows, :].astype(BF16)


def query_block(step, core, seq, len_ref, got_ref, diag_e_ref, diag_dp_ref, diag_stat_ref, out_ref, k_ref, v_ref, kt_ref, e_ref, dp_ref, dk_ref, dv_ref):
    block = step * CORES + core
    place, begin, first_begin = documents(block, seq, len_ref)
    low = first_begin // OWN

    q_rows, g_rows, q_cols, g_cols = queries(step, got_ref)

    def window(count):
        tops, masses, sums = [], [], []
        if count > 1:
            keys = pl.ds(pl.multiple_of(low * OWN, OWN), (count - 1) * OWN)
            s_all = jnp.dot(k_ref[keys, :], q_cols, preferred_element_type=F32)
            dp_all = jnp.dot(v_ref[keys, :], g_cols, preferred_element_type=F32)
        for r in range(count - 1):
            rs = slice(r * OWN, (r + 1) * OWN)
            e, top, mass, weighted = weigh(s_all[rs], dp_all[rs], key_places(low + r) >= begin)
            e_ref[rs] = e
            dp_ref[rs] = dp_all[rs]
            tops.append(top)
            masses.append(mass)
            sums.append(weighted)
        tops.append(diag_stat_ref[step, 0])
        masses.append(diag_stat_ref[step, 1])
        sums.append(diag_stat_ref[step, 2])

        def kept(ref, diag_ref, r):
            held = diag_ref[step] if r == count - 1 else ref[r * OWN : (r + 1) * OWN]
            return held.reshape(OWN // 8, 8, WIDTH)

        peak = jnp.max(functools.reduce(jnp.maximum, tops), axis=0, keepdims=True)
        scales = [jnp.exp2(top - peak) for top in tops]
        mass = sum(m * f for m, f in zip(masses, scales))
        weighted = sum(m * f for m, f in zip(sums, scales))
        inverse = 1.0 / jnp.sum(mass, axis=0, keepdims=True)
        delta = jnp.sum(weighted, axis=0, keepdims=True) * inverse
        inverse = jnp.broadcast_to(inverse, (8, WIDTH))
        delta = jnp.broadcast_to(delta, (8, WIDTH))
        dq = None
        done = 0
        while done < count:
            size = (count - done) % 4 or 4
            low_probs, ds = [], []
            for r in range(done, done + size):
                p = kept(e_ref, diag_e_ref, r) * (scales[r] * inverse)[None]
                d = p * (kept(dp_ref, diag_dp_ref, r) - delta[None])
                low_probs.append(p.reshape(OWN, WIDTH).astype(BF16))
                ds.append(d.reshape(OWN, WIDTH).astype(BF16))
            low_probs = jnp.concatenate(low_probs, axis=0)
            ds = jnp.concatenate(ds, axis=0)
            rows = pl.ds(pl.multiple_of((low + done) * OWN, OWN), size * OWN)
            dv_ref[rows, :] += jnp.dot(low_probs, g_rows, preferred_element_type=F32)
            dk_ref[rows, :] += jnp.dot(ds, q_rows, preferred_element_type=F32)
            kt = jnp.concatenate([kt_ref[low + done + i] for i in range(size)], axis=1)
            part = jnp.dot(kt, ds, preferred_element_type=F32)
            dq = part if dq is None else dq + part
            done += size
        dq = (dq * SCALE).astype(BF16).T
        for h in range(HEADS):
            out_ref[out_slot(step), :, h * DH : (h + 1) * DH] = dq[h * OWN : (h + 1) * OWN]

    for count in range(1, MOST + 1):
        pl.when(block - low + 1 == count)(functools.partial(window, count))

def attention(own, assignment, doc_lengths, rows, other, diag):
    small = pl.BlockSpec(memory_space=pltpu.SMEM)
    large = pl.BlockSpec(memory_space=pltpu.VMEM)
    return pl.pallas_call(
        attention_kernel,
        out_shape=(
            jax.ShapeDtypeStruct((CHIPS, OWN, OUT_W), BF16),
            jax.ShapeDtypeStruct((CHIPS, OWN, 2 * DH), BF16),
        ),
        in_specs=[small, small, small] + [large] * 5,
        out_specs=(large, large),
        scratch_shapes=[
            pltpu.VMEM((LEN, DH), BF16),
            pltpu.VMEM((LEN, DH), BF16),
            pltpu.VMEM((BLOCKS, DH, OWN), BF16),
            pltpu.VMEM(((MOST - 1) * OWN, WIDTH), F32),
            pltpu.VMEM(((MOST - 1) * OWN, WIDTH), F32),
            pltpu.VMEM((LEN, DH), F32),
            pltpu.VMEM((LEN, DH), F32),
        ],
        compiler_params=pltpu.CompilerParams(vmem_limit_bytes=40 * MIB),
        name="attention",
    )(own, assignment, doc_lengths, rows, other, *diag)


def add_kernel(a_ref, b_ref, out_ref):
    out_ref[...] = (a_ref[...].astype(F32) + b_ref[...].astype(F32)).astype(BF16)


def add_partials(grads, given):
    some = CHIPS // 4
    tail = pl.BlockSpec((some, OWN, 2 * DH), lambda i: (i, 0, QW // (2 * DH)))
    return pl.pallas_call(
        add_kernel,
        out_shape=jax.ShapeDtypeStruct(grads.shape, BF16),
        grid=(CHIPS // some,),
        in_specs=[tail, pl.BlockSpec((some, OWN, 2 * DH), lambda i: (i, 0, 0))],
        out_specs=tail,
        input_output_aliases={0: 0},
        compiler_params=pltpu.CompilerParams(vmem_limit_bytes=8 * MIB),
        name="add_partials",
    )(grads, given)


def unpack_kernel(in_ref, dq_hbm, dk_hbm, dv_hbm, dq_ref, dk_ref, dv_ref, out_sem, thin_sem):
    stores = []
    for i in range(OWN // PIECE):
        rows = slice(i * PIECE, (i + 1) * PIECE)
        for chip in range(CHIPS):
            dq_ref[0, rows, chip * QW : (chip + 1) * QW] = in_ref[out_slot(chip), rows, 0:QW]
        move = pltpu.make_async_copy(dq_ref.at[:, rows], dq_hbm.at[:, rows], out_sem.at[i])
        move.start()
        stores.append(move)
    for j in range(HK):
        dk = jnp.zeros((OWN, DH), F32)
        dv = jnp.zeros((OWN, DH), F32)
        for chip in range(j * SHARE, (j + 1) * SHARE):
            dk = dk + in_ref[out_slot(chip), :, QW : QW + DH].astype(F32)
            dv = dv + in_ref[out_slot(chip), :, QW + DH : OUT_W].astype(F32)
        dk_ref[0, :, j * DH : (j + 1) * DH] = dk.astype(BF16)
        dv_ref[0, :, j * DH : (j + 1) * DH] = dv.astype(BF16)
    for a, (held, target) in enumerate(((dk_ref, dk_hbm), (dv_ref, dv_hbm))):
        move = pltpu.make_async_copy(held, target, thin_sem.at[a])
        move.start()
        stores.append(move)
    for move in stores:
        move.wait()


def unpack(blocks):
    return pl.pallas_call(
        unpack_kernel,
        out_shape=(
            jax.ShapeDtypeStruct((1, OWN, HQ * DH), BF16),
            jax.ShapeDtypeStruct((1, OWN, HK * DH), BF16),
            jax.ShapeDtypeStruct((1, OWN, HK * DH), BF16),
        ),
        in_specs=[pl.BlockSpec(memory_space=pltpu.VMEM)],
        out_specs=(
            pl.BlockSpec(memory_space=pl.ANY),
            pl.BlockSpec(memory_space=pl.ANY),
            pl.BlockSpec(memory_space=pl.ANY),
        ),
        scratch_shapes=[
            pltpu.VMEM((1, OWN, HQ * DH), BF16),
            pltpu.VMEM((1, OWN, HK * DH), BF16),
            pltpu.VMEM((1, OWN, HK * DH), BF16),
            pltpu.SemaphoreType.DMA((OWN // PIECE,)),
            pltpu.SemaphoreType.DMA((2,)),
        ],
        compiler_params=pltpu.CompilerParams(vmem_limit_bytes=24 * MIB),
        name="unpack",
    )(blocks)


def swap_cores(x):
    return lax.ppermute(x, "core", [(0, 1), (1, 0)])


def local(query_rows, key_rows, value_rows, out_grad, doc_lengths, assignment):
    own = jnp.stack([lax.axis_index(DP_AXES), lax.axis_index("core")]).astype(jnp.int32)
    sent = pack(assignment, query_rows, out_grad, key_rows, value_rows).reshape(CHIPS * DP, ROWS, IN_W)
    got = lax.all_to_all(sent, IN_AXES, split_axis=0, concat_axis=0, tiled=True)
    rows = got.reshape(X, Z, Y_HI, Y_LO * ROWS, IN_W)
    other = swap_cores(rows[..., 2 * QW : IN_W])
    diag = diagonal(own, assignment, doc_lengths, rows)
    grads, give = attention(own, assignment, doc_lengths, rows, other, diag)
    grads = add_partials(grads, swap_cores(give))
    back = lax.all_to_all(grads, OUT_AXES, split_axis=0, concat_axis=0, tiled=True)
    return unpack(back)


def solution(mesh):
    fine = Mesh(mesh.devices.reshape(Y_HI, Z, CORES, X, Y_LO), CTX_AXES + DP_AXES)
    placed = P(None, CTX_AXES + DP_AXES, None)
    return jax.shard_map(
        local,
        mesh=fine,
        in_specs=(placed, placed, placed, placed, P(), P()),
        out_specs=(P(DP_AXES, CTX_AXES, None),) * 3,
        check_vma=False,
    )
```

```python
import functools
import math

import jax
import jax.numpy as jnp
from jax import lax
from jax.experimental import pallas as pl
from jax.experimental.pallas import tpu as pltpu
from jax.sharding import Mesh, PartitionSpec as P

HQ = 32
HK = 4
DH = 128
NDOC = 8
LEN = 2048

Y_HI, Z, CORES, X, Y_LO = 2, 4, 2, 4, 2
CTX_AXES = ("y_hi", "z", "core")
DP_AXES = ("x", "y_lo")
IN_AXES = ("x", "z", "y_hi", "y_lo")
OUT_AXES = ("y_hi", "z")
CTX = Y_HI * Z * CORES
DP = X * Y_LO
CHIPS = Y_HI * Z
ROWS = LEN // (CTX * DP)
OWN = LEN // CTX
HEADS = HQ // CHIPS
QW = HEADS * DH
SHARE = CHIPS // HK
IN_W = 2 * QW + 2 * DH
OUT_W = QW + 2 * DH
PIECE = 32
UNROLL = 8

WIDTH = HEADS * OWN
BLOCKS = LEN // OWN
MOST = (LEN // 2 + OWN - 2) // OWN + 1

SCALE = DH ** (-0.5)
LOG2E = math.log2(math.e)
MASKED = -1e30
F32 = jnp.float32
BF16 = jnp.bfloat16
MIB = 1024 * 1024


def out_slot(chip):
    return chip


def pack_kernel(seq_ref, q_in, g_in, k_in, v_in, out, q_ref, g_ref, k_ref, v_ref, out_ref, in_sem, out_sem):
    wide = SHARE * QW

    def load(j, a, source, held, width):
        cols = slice(j * width, (j + 1) * width)
        return pltpu.make_async_copy(source.at[:, :, cols], held.at[:, :, cols], in_sem.at[j, a])

    loads = [
        [load(j, 0, q_in, q_ref, wide), load(j, 1, g_in, g_ref, wide), load(j, 2, k_in, k_ref, DH), load(j, 3, v_in, v_ref, DH)]
        for j in range(HK)
    ]
    for group in loads:
        for move in group:
            move.start()
    stores = []
    for j in range(HK):
        for move in loads[j]:
            move.wait()
        thin = slice(j * DH, (j + 1) * DH)
        for chip in range(j * SHARE, (j + 1) * SHARE):
            cols = slice(chip * QW, (chip + 1) * QW)
            y_hi, z = chip // Z, chip % Z
            for group in range(DP):
                seq = seq_ref[group]
                x, y_lo = group // Y_LO, group % Y_LO
                out_ref[x, z, y_hi, y_lo, :, 0:QW] = q_ref[seq, :, cols]
                out_ref[x, z, y_hi, y_lo, :, QW : 2 * QW] = g_ref[seq, :, cols]
                out_ref[x, z, y_hi, y_lo, :, 2 * QW : 2 * QW + DH] = k_ref[seq, :, thin]
                out_ref[x, z, y_hi, y_lo, :, 2 * QW + DH : IN_W] = v_ref[seq, :, thin]
            move = pltpu.make_async_copy(out_ref.at[:, z, y_hi], out.at[:, z, y_hi], out_sem.at[chip])
            move.start()
            stores.append(move)
    for move in stores:
        move.wait()


def pack(assignment, query_rows, out_grad, key_rows, value_rows):
    whole = pl.BlockSpec(memory_space=pl.ANY)
    shape = (X, Z, Y_HI, Y_LO, ROWS, IN_W)
    return pl.pallas_call(
        pack_kernel,
        out_shape=jax.ShapeDtypeStruct(shape, BF16),
        in_specs=[pl.BlockSpec(memory_space=pltpu.SMEM)] + [whole] * 4,
        out_specs=whole,
        scratch_shapes=[
            pltpu.VMEM((DP, ROWS, HQ * DH), BF16),
            pltpu.VMEM((DP, ROWS, HQ * DH), BF16),
            pltpu.VMEM((DP, ROWS, HK * DH), BF16),
            pltpu.VMEM((DP, ROWS, HK * DH), BF16),
            pltpu.VMEM(shape, BF16),
            pltpu.SemaphoreType.DMA((HK, 4)),
            pltpu.SemaphoreType.DMA((CHIPS,)),
        ],
        compiler_params=pltpu.CompilerParams(vmem_limit_bytes=60 * MIB),
        name="pack",
    )(assignment, query_rows, out_grad, key_rows, value_rows)


def block_rows(block):
    return pl.ds(pl.multiple_of(block * OWN, OWN), OWN)


def documents(block, seq, len_ref):
    first = block * OWN
    place = first + lax.broadcasted_iota(jnp.int32, (1, OWN), 1)
    begin = jnp.zeros((1, OWN), jnp.int32)
    first_begin = jnp.int32(0)
    end = jnp.int32(0)
    for j in range(NDOC):
        end = end + len_ref[seq, j]
        begin = jnp.where(place >= end, end, begin)
        first_begin = jnp.where(first >= end, end, first_begin)
    place = jnp.concatenate([place] * HEADS, axis=1)
    begin = jnp.concatenate([begin] * HEADS, axis=1)
    return place, begin, first_begin


def queries(step, got_ref):
    qg = got_ref[:, step % Z, step // Z, :, 0 : 2 * QW].reshape(OWN, 2 * QW)
    q_rows = jnp.concatenate([qg[:, h * DH : (h + 1) * DH] for h in range(HEADS)], axis=0)
    g_rows = jnp.concatenate([qg[:, QW + h * DH : QW + (h + 1) * DH] for h in range(HEADS)], axis=0)
    q_cols = q_rows.T
    g_cols = g_rows.T
    return q_rows, g_rows, q_cols, g_cols


def weigh(s, dp, seen):
    s = jnp.where(seen, s * (SCALE * LOG2E), MASKED).reshape(OWN // 8, 8, WIDTH)
    top = jnp.max(s, axis=0)
    e = jnp.exp2(s - top[None])
    return e.reshape(OWN, WIDTH), top, jnp.sum(e, axis=0), jnp.sum(e * dp.reshape(OWN // 8, 8, WIDTH), axis=0)


def key_places(block):
    return block * OWN + lax.broadcasted_iota(jnp.int32, (OWN, WIDTH), 0)


def diagonal_kernel(own_ref, seq_ref, len_ref, got_ref, e_ref, dp_ref, stat_ref):
    seq = seq_ref[own_ref[0]]
    core = own_ref[1]

    def one_block(step, _):
        block = step * CORES + core
        place, begin, _first = documents(block, seq, len_ref)
        _q, _g, q_cols, g_cols = queries(step, got_ref)
        kv = got_ref[:, step % Z, step // Z, :, 2 * QW : IN_W].reshape(OWN, 2 * DH)
        s = jnp.dot(kv[:, 0:DH], q_cols, preferred_element_type=F32)
        dp = jnp.dot(kv[:, DH : 2 * DH], g_cols, preferred_element_type=F32)
        u = key_places(block)
        e, top, mass, weighted = weigh(s, dp, (u >= begin) & (u <= place))
        e_ref[step] = e
        dp_ref[step] = dp
        stat_ref[step, 0] = top
        stat_ref[step, 1] = mass
        stat_ref[step, 2] = weighted
        return 0

    lax.fori_loop(0, CHIPS, one_block, 0, unroll=UNROLL)


def diagonal(own, assignment, doc_lengths, rows):
    small = pl.BlockSpec(memory_space=pltpu.SMEM)
    large = pl.BlockSpec(memory_space=pltpu.VMEM)
    return pl.pallas_call(
        diagonal_kernel,
        out_shape=(
            jax.ShapeDtypeStruct((CHIPS, OWN, WIDTH), F32),
            jax.ShapeDtypeStruct((CHIPS, OWN, WIDTH), F32),
            jax.ShapeDtypeStruct((CHIPS, 3, 8, WIDTH), F32),
        ),
        in_specs=[small, small, small, large],
        out_specs=(large, large, large),
        compiler_params=pltpu.CompilerParams(vmem_limit_bytes=24 * MIB),
        cost_estimate=pl.CostEstimate(
            flops=4 * CHIPS * OWN * WIDTH * DH, bytes_accessed=8 * MIB, transcendentals=CHIPS * OWN * WIDTH
        ),
        name="diagonal",
    )(own, assignment, doc_lengths, rows)


def attention_kernel(
    own_ref, seq_ref, len_ref, got_ref, other_ref, diag_e_ref, diag_dp_ref, diag_stat_ref, out_ref, give_ref, k_ref, v_ref, kt_ref, e_ref, dp_ref, dk_ref, dv_ref
):
    seq = seq_ref[own_ref[0]]
    core = own_ref[1]
    dk_ref[...] = jnp.zeros_like(dk_ref)
    dv_ref[...] = jnp.zeros_like(dv_ref)
    for chip in range(CHIPS):
        place = (slice(None), chip % Z, chip // Z)
        mine = got_ref[(*place, slice(None), slice(2 * QW, IN_W))]
        for got, got_core in ((mine, core), (other_ref[place], 1 - core)):
            got = got.reshape(OWN, 2 * DH)
            rows = block_rows(chip * CORES + got_core)
            k_ref[rows, :] = got[:, 0:DH]
            v_ref[rows, :] = got[:, DH : 2 * DH]
            kt_ref[chip * CORES + got_core] = got[:, 0:DH].T

    def one_block(step, _):
        query_block(step, core, seq, len_ref, got_ref, diag_e_ref, diag_dp_ref, diag_stat_ref, out_ref, k_ref, v_ref, kt_ref, e_ref, dp_ref, dk_ref, dv_ref)
        return _

    lax.fori_loop(0, CHIPS, one_block, 0)
    for chip in range(CHIPS):
        slot = out_slot(chip)
        rows = block_rows(chip * CORES + core)
        out_ref[slot, :, QW : QW + DH] = (dk_ref[rows, :] * SCALE).astype(BF16)
        out_ref[slot, :, QW + DH : OUT_W] = dv_ref[rows, :].astype(BF16)
        rows = block_rows(chip * CORES + 1 - core)
        give_ref[slot, :, 0:DH] = (dk_ref[rows, :] * SCALE).astype(BF16)
        give_ref[slot, :, DH : 2 * DH] = dv_ref[rows, :].astype(BF16)


def query_block(step, core, seq, len_ref, got_ref, diag_e_ref, diag_dp_ref, diag_stat_ref, out_ref, k_ref, v_ref, kt_ref, e_ref, dp_ref, dk_ref, dv_ref):
    block = step * CORES + core
    place, begin, first_begin = documents(block, seq, len_ref)
    low = first_begin // OWN

    q_rows, g_rows, q_cols, g_cols = queries(step, got_ref)

    def window(count):
        tops, masses, sums = [], [], []
        if count > 1:
            keys = pl.ds(pl.multiple_of(low * OWN, OWN), (count - 1) * OWN)
            s_all = jnp.dot(k_ref[keys, :], q_cols, preferred_element_type=F32)
            dp_all = jnp.dot(v_ref[keys, :], g_cols, preferred_element_type=F32)
        for r in range(count - 1):
            rs = slice(r * OWN, (r + 1) * OWN)
            e, top, mass, weighted = weigh(s_all[rs], dp_all[rs], key_places(low + r) >= begin)
            e_ref[rs] = e
            dp_ref[rs] = dp_all[rs]
            tops.append(top)
            masses.append(mass)
            sums.append(weighted)
        tops.append(diag_stat_ref[step, 0])
        masses.append(diag_stat_ref[step, 1])
        sums.append(diag_stat_ref[step, 2])

        def kept(ref, diag_ref, r):
            held = diag_ref[step] if r == count - 1 else ref[r * OWN : (r + 1) * OWN]
            return held.reshape(OWN // 8, 8, WIDTH)

        peak = jnp.max(functools.reduce(jnp.maximum, tops), axis=0, keepdims=True)
        scales = [jnp.exp2(top - peak) for top in tops]
        mass = sum(m * f for m, f in zip(masses, scales))
        weighted = sum(m * f for m, f in zip(sums, scales))
        inverse = 1.0 / jnp.sum(mass, axis=0, keepdims=True)
        delta = jnp.sum(weighted, axis=0, keepdims=True) * inverse
        inverse = jnp.broadcast_to(inverse, (8, WIDTH))
        delta = jnp.broadcast_to(delta, (8, WIDTH))
        dq = None
        done = 0
        while done < count:
            size = (count - done) % 4 or 4
            low_probs, ds = [], []
            for r in range(done, done + size):
                p = kept(e_ref, diag_e_ref, r) * (scales[r] * inverse)[None]
                d = p * (kept(dp_ref, diag_dp_ref, r) - delta[None])
                low_probs.append(p.reshape(OWN, WIDTH).astype(BF16))
                ds.append(d.reshape(OWN, WIDTH).astype(BF16))
            low_probs = jnp.concatenate(low_probs, axis=0)
            ds = jnp.concatenate(ds, axis=0)
            rows = pl.ds(pl.multiple_of((low + done) * OWN, OWN), size * OWN)
            dv_ref[rows, :] += jnp.dot(low_probs, g_rows, preferred_element_type=F32)
            dk_ref[rows, :] += jnp.dot(ds, q_rows, preferred_element_type=F32)
            kt = jnp.concatenate([kt_ref[low + done + i] for i in range(size)], axis=1)
            part = jnp.dot(kt, ds, preferred_element_type=F32)
            dq = part if dq is None else dq + part
            done += size
        dq = (dq * SCALE).astype(BF16).T
        for h in range(HEADS):
            out_ref[out_slot(step), :, h * DH : (h + 1) * DH] = dq[h * OWN : (h + 1) * OWN]

    for count in range(1, MOST + 1):
        pl.when(block - low + 1 == count)(functools.partial(window, count))

def attention(own, assignment, doc_lengths, rows, other, diag):
    small = pl.BlockSpec(memory_space=pltpu.SMEM)
    large = pl.BlockSpec(memory_space=pltpu.VMEM)
    return pl.pallas_call(
        attention_kernel,
        out_shape=(
            jax.ShapeDtypeStruct((CHIPS, OWN, OUT_W), BF16),
            jax.ShapeDtypeStruct((CHIPS, OWN, 2 * DH), BF16),
        ),
        in_specs=[small, small, small] + [large] * 5,
        out_specs=(large, large),
        scratch_shapes=[
            pltpu.VMEM((LEN, DH), BF16),
            pltpu.VMEM((LEN, DH), BF16),
            pltpu.VMEM((BLOCKS, DH, OWN), BF16),
            pltpu.VMEM(((MOST - 1) * OWN, WIDTH), F32),
            pltpu.VMEM(((MOST - 1) * OWN, WIDTH), F32),
            pltpu.VMEM((LEN, DH), F32),
            pltpu.VMEM((LEN, DH), F32),
        ],
        compiler_params=pltpu.CompilerParams(vmem_limit_bytes=40 * MIB),
        name="attention",
    )(own, assignment, doc_lengths, rows, other, *diag)


def add_kernel(a_ref, b_ref, out_ref):
    out_ref[...] = (a_ref[...].astype(F32) + b_ref[...].astype(F32)).astype(BF16)


def add_partials(grads, given):
    some = CHIPS // 4
    tail = pl.BlockSpec((some, OWN, 2 * DH), lambda i: (i, 0, QW // (2 * DH)))
    return pl.pallas_call(
        add_kernel,
        out_shape=jax.ShapeDtypeStruct(grads.shape, BF16),
        grid=(CHIPS // some,),
        in_specs=[tail, pl.BlockSpec((some, OWN, 2 * DH), lambda i: (i, 0, 0))],
        out_specs=tail,
        input_output_aliases={0: 0},
        compiler_params=pltpu.CompilerParams(vmem_limit_bytes=8 * MIB),
        name="add_partials",
    )(grads, given)


def unpack_kernel(in_ref, dq_hbm, dk_hbm, dv_hbm, dq_ref, dk_ref, dv_ref, out_sem, thin_sem):
    stores = []
    for i in range(OWN // PIECE):
        rows = slice(i * PIECE, (i + 1) * PIECE)
        for chip in range(CHIPS):
            dq_ref[0, rows, chip * QW : (chip + 1) * QW] = in_ref[out_slot(chip), rows, 0:QW]
        move = pltpu.make_async_copy(dq_ref.at[:, rows], dq_hbm.at[:, rows], out_sem.at[i])
        move.start()
        stores.append(move)
    for j in range(HK):
        dk = jnp.zeros((OWN, DH), F32)
        dv = jnp.zeros((OWN, DH), F32)
        for chip in range(j * SHARE, (j + 1) * SHARE):
            dk = dk + in_ref[out_slot(chip), :, QW : QW + DH].astype(F32)
            dv = dv + in_ref[out_slot(chip), :, QW + DH : OUT_W].astype(F32)
        dk_ref[0, :, j * DH : (j + 1) * DH] = dk.astype(BF16)
        dv_ref[0, :, j * DH : (j + 1) * DH] = dv.astype(BF16)
    for a, (held, target) in enumerate(((dk_ref, dk_hbm), (dv_ref, dv_hbm))):
        move = pltpu.make_async_copy(held, target, thin_sem.at[a])
        move.start()
        stores.append(move)
    for move in stores:
        move.wait()


def unpack(blocks):
    return pl.pallas_call(
        unpack_kernel,
        out_shape=(
            jax.ShapeDtypeStruct((1, OWN, HQ * DH), BF16),
            jax.ShapeDtypeStruct((1, OWN, HK * DH), BF16),
            jax.ShapeDtypeStruct((1, OWN, HK * DH), BF16),
        ),
        in_specs=[pl.BlockSpec(memory_space=pltpu.VMEM)],
        out_specs=(
            pl.BlockSpec(memory_space=pl.ANY),
            pl.BlockSpec(memory_space=pl.ANY),
            pl.BlockSpec(memory_space=pl.ANY),
        ),
        scratch_shapes=[
            pltpu.VMEM((1, OWN, HQ * DH), BF16),
            pltpu.VMEM((1, OWN, HK * DH), BF16),
            pltpu.VMEM((1, OWN, HK * DH), BF16),
            pltpu.SemaphoreType.DMA((OWN // PIECE,)),
            pltpu.SemaphoreType.DMA((2,)),
        ],
        compiler_params=pltpu.CompilerParams(vmem_limit_bytes=24 * MIB),
        name="unpack",
    )(blocks)


def swap_cores(x):
    return lax.ppermute(x, "core", [(0, 1), (1, 0)])


def local(query_rows, key_rows, value_rows, out_grad, doc_lengths, assignment):
    own = jnp.stack([lax.axis_index(DP_AXES), lax.axis_index("core")]).astype(jnp.int32)
    sent = pack(assignment, query_rows, out_grad, key_rows, value_rows).reshape(CHIPS * DP, ROWS, IN_W)
    got = lax.all_to_all(sent, IN_AXES, split_axis=0, concat_axis=0, tiled=True)
    rows = got.reshape(X, Z, Y_HI, Y_LO * ROWS, IN_W)
    other = swap_cores(rows[..., 2 * QW : IN_W])
    diag = diagonal(own, assignment, doc_lengths, rows)
    grads, give = attention(own, assignment, doc_lengths, rows, other, diag)
    grads = add_partials(grads, swap_cores(give))
    back = lax.all_to_all(grads, OUT_AXES, split_axis=0, concat_axis=0, tiled=True)
    return unpack(back)


def solution(mesh):
    fine = Mesh(mesh.devices.reshape(Y_HI, Z, CORES, X, Y_LO), CTX_AXES + DP_AXES)
    placed = P(None, CTX_AXES + DP_AXES, None)
    return jax.shard_map(
        local,
        mesh=fine,
        in_specs=(placed, placed, placed, placed, P(), P()),
        out_specs=(P(DP_AXES, CTX_AXES, None),) * 3,
        check_vma=False,
    )
```
